32 devices in a mesh: gx: 4 (over z), gy: 8 (over y, x, core).
Axes of the slice: x: 2, y: 2, z: 4, core: 2. Of those that a mesh axis runs over, the one named last changes fastest.
Arguments:
- coupling: bfloat16 [4, 64, 1024, 512], P('gx', 'gy'), may hold values from -0.44921875 to 0.44921875
- local_block: bfloat16 [4, 64, 512, 512], P('gx', 'gy'), as said below
- counts: int32 [4, 64], P('gx', 'gy'), may hold values from 1 to 4, as said below
- primal: int32 [4, 64, 512], P('gx', 'gy'), may hold values from 0 to 511
- partner: int32 [3, 4], replicated, may hold values from 0 to 3, as said below
Outputs:
- coarse: float32 [4, 512, 512], P('gx')
The draws below stay inside these ranges and needn't reach their ends.
Inputs may be any that keep to these rules, and one draw needn't show every extreme that they name: Each row of partner is a perfect matching of the 4 columns: partner[r, partner[r, c]] == c and partner[r, c] != c. `counts`: in each subdomain column at least one subdomain has all 4 blocks live. `primal`: any constraint may hold any number of rows. `local_block`: diagonal entries are positive.
All inputs are finite; a program needn't handle non-finite values. Where the reference program divides by a largest or mean magnitude, that divisor is 1e-20 or more.
Results may differ from the reference program's by a relative error of at most 0.00078.
Values sent between devices are 32-bit elements; how exact they have to be, the bound alone decides.
No kernel may reach another device: no remote copies, remote signals or barrier semaphores. Data moves between devices by JAX's collectives and lax.ppermute only.
A program may use at most 192 MiB of HBM per device.

```python
import math
import jax
import jax.numpy as jnp
from jax import lax

BLK = 128
RB = 4
NI = 1024
NC = 512
ROUNDS = 3
R = 512
NCOL = 4
SUBS = 64


def draw_local_block(key, part):
    first, second = jax.random.split(key)
    shape = (NCOL, SUBS, R, R)
    off = 0.3 * jax.random.normal(first, shape, jnp.float32)
    lead = jnp.exp(jax.random.uniform(second, shape, jnp.float32, math.log(2.0), math.log(20.0)))
    rows = lax.broadcasted_iota(jnp.int32, shape, 2)
    cols = lax.broadcasted_iota(jnp.int32, shape, 3)
    return jnp.where(rows == cols, lead, off).astype(jnp.bfloat16)


def draw_counts(key, part):
    drawn = jax.random.randint(key, (NCOL, SUBS), 1, RB + 1)
    col = lax.broadcasted_iota(jnp.int32, (NCOL, SUBS), 0)
    sub = lax.broadcasted_iota(jnp.int32, (NCOL, SUBS), 1)
    full = sub == (col * 3 + 1) % SUBS
    return jnp.where(full, RB, drawn).astype(jnp.int32)


def draw_partner(key, part):

    def single(round_key):
        order = jax.random.permutation(round_key, NCOL).astype(jnp.int32)
        place = jnp.argsort(order, stable=True).astype(jnp.int32)
        return order[jnp.bitwise_xor(place, 1)]
    keys = jax.random.split(key, ROUNDS)
    return jax.vmap(single)(keys).astype(jnp.int32)


def set_ends(entries, own_key, least, top_value):
    shape = entries.shape
    spot = [jax.random.randint(jax.random.fold_in(own_key, axis), (), 0, shape[axis]) for axis in range(len(shape))]
    entries = entries.at[tuple(spot)].set(least)
    longest = shape.index(max(shape))
    spot[longest] = (spot[longest] + 1) % shape[longest]
    return entries.at[tuple(spot)].set(top_value)


def level_of(rng, extent, pieces, smallest, top_value):
    gain = 1.0
    for dim, blocks in pieces:
        heights = jax.random.uniform(jax.random.fold_in(jax.random.fold_in(rng, 6), dim), (blocks,), jnp.float32, smallest / len(pieces), top_value / len(pieces))
        gain = gain * jnp.repeat(jnp.exp(heights), extent[dim] // blocks).reshape((-1,) + (1,) * (len(extent) - 1 - dim))
    return gain


def normal_values(rng, shape, width, bound, pieces=(), kind=jnp.bfloat16):
    entries = jax.random.normal(rng, shape, jnp.float32) * width
    if len(pieces) > 0:
        entries = level_of(rng, shape, pieces, -0.22, 0.18) * entries
    return jnp.clip(entries, min=-bound, max=bound).astype(kind)


def setup_inputs(seed: int = 0) -> dict:
    streams_of = jax.random.split(jax.random.key(seed), 6)
    return {
        "coupling": normal_values(streams_of[0], (NCOL, SUBS, NI, R), 0.0766, 0.44921875, ((0, 4), (1, 8))),
        "local_block": draw_local_block(jax.random.fold_in(streams_of[5], 71), 0),
        "counts": draw_counts(jax.random.fold_in(streams_of[5], 71), 0),
        "primal": set_ends(jax.random.randint(streams_of[3], (NCOL, SUBS, R), 0, NC), jax.random.fold_in(streams_of[3], 1), 0, NC - 1).astype(jnp.int32),
        "partner": draw_partner(jax.random.fold_in(streams_of[5], 71), 0),
    }


def contribution(coupling_s, block_s, count_s, prim_s, weight_s):
    rows = jnp.arange(R, dtype=jnp.int32)
    live = (rows < count_s * BLK).astype(jnp.float32)
    gram = jnp.dot(coupling_s.T, coupling_s, preferred_element_type=jnp.float32)
    schur = ((block_s.astype(jnp.float32) - gram) * live[:, None] * live[None, :]).astype(jnp.bfloat16)
    onehot = prim_s[:, None] == jnp.arange(NC, dtype=jnp.int32)[None, :]
    basis = jnp.where(onehot, weight_s[:, None], jnp.zeros((), jnp.float32)).astype(jnp.bfloat16)
    image = jnp.dot(schur, basis, preferred_element_type=jnp.float32).astype(jnp.bfloat16)
    return jnp.dot(basis.T, image, preferred_element_type=jnp.float32)

def reference(coupling, local_block, counts, primal, partner):
    stiff = jnp.diagonal(local_block, axis1=2, axis2=3).astype(jnp.float32)
    total = stiff
    for r in range(ROUNDS):
        total = total + stiff[partner[r]]
    weight = stiff / total

    def column(c):

        def step(acc, j):
            term = contribution(coupling[c, j], local_block[c, j], counts[c, j], primal[c, j], weight[c, j])
            return (acc + term, None)
        acc, _ = lax.scan(step, jnp.zeros((NC, NC), jnp.float32), jnp.arange(SUBS, dtype=jnp.int32))
        return acc
    tiles = lax.map(column, jnp.arange(NCOL, dtype=jnp.int32))
    scale = 1.0 / jnp.sqrt(lax.optimization_barrier(jnp.mean(jnp.abs(tiles), axis=2)) + 1e-06)
    return tiles * scale[:, :, None] * scale[:, None, :]
```

```python
import functools

import jax
import jax.numpy as jnp
from jax import lax
from jax.experimental import pallas as pl
from jax.experimental.pallas import tpu as pltpu
from jax.sharding import PartitionSpec as P

BLK = 128
NC = 512
ROUNDS = 3
R = 512
NI = 1024
RB = 4
VMEM_LIMIT = 24 << 20

F32 = jnp.float32
BF16 = jnp.bfloat16


def params():
    return pltpu.CompilerParams(vmem_limit_bytes=VMEM_LIMIT)


def in_vmem(*arrays):
    return [pltpu.with_memory_space_constraint(a, pltpu.VMEM) for a in arrays]


VSPEC = pl.BlockSpec(memory_space=pltpu.VMEM)
SSPEC = pl.BlockSpec(memory_space=pltpu.SMEM)
ASPEC = pl.BlockSpec(memory_space=pl.ANY)


def diag_kernel(block_ref, stiff_ref, held, sems):
    def copy(b):
        part = pl.ds(b * BLK, BLK)
        return pltpu.make_async_copy(block_ref.at[:, part, part], held.at[b], sems.at[b])

    for b in range(RB):
        copy(b).start()
    shape = (BLK, BLK)
    on = lax.broadcasted_iota(jnp.int32, shape, 0) == lax.broadcasted_iota(jnp.int32, shape, 1)
    for b in range(RB):
        copy(b).wait()
        tile = held[b].astype(F32)
        stiff_ref[:, b * BLK : (b + 1) * BLK] = jnp.sum(jnp.where(on[None], tile, 0.0), axis=1)


def diagonal(local_block):
    subs = local_block.shape[0]
    return pl.pallas_call(
        diag_kernel,
        out_shape=pltpu.VMEM((subs, R), F32),
        in_specs=[ASPEC],
        out_specs=VSPEC,
        scratch_shapes=[pltpu.VMEM((RB, subs, BLK, BLK), BF16), pltpu.SemaphoreType.DMA((RB,))],
        compiler_params=params(),
        name="diag",
    )(pltpu.with_memory_space_constraint(local_block, pltpu.HBM))


def schur_kernel(counts_ref, coupling_ref, block_ref, schur_ref):
    j = pl.program_id(0)
    for live in range(1, RB + 1):

        @pl.when(counts_ref[j] == live)
        def _():
            n = live * BLK
            c = coupling_ref[0, :, :n]
            gram = lax.dot_general(c, c, (((0,), (0,)), ((), ())), preferred_element_type=F32)
            schur_ref[0, :n, :n] = (block_ref[0, :n, :n].astype(F32) - gram).astype(BF16)
            if n < R:
                schur_ref[0, :n, n:] = jnp.zeros((n, R - n), BF16)
                schur_ref[0, n:, :] = jnp.zeros((R - n, R), BF16)


def schur_blocks(counts, coupling, local_block):
    subs = local_block.shape[0]
    return pl.pallas_call(
        schur_kernel,
        grid_spec=pltpu.PrefetchScalarGridSpec(
            num_scalar_prefetch=1,
            grid=(subs,),
            in_specs=[
                pl.BlockSpec((1, NI, R), lambda j, c: (j, 0, 0)),
                pl.BlockSpec((1, R, R), lambda j, c: (j, 0, 0)),
            ],
            out_specs=pl.BlockSpec((1, R, R), lambda j, c: (j, 0, 0)),
        ),
        out_shape=pltpu.VMEM((subs, R, R), BF16),
        compiler_params=params(),
        name="schur",
    )(counts, coupling, local_block)


def first_kernel(half, off_ref, times_ref, primal_ref, stiff_ref, *refs):
    *others, schur_ref, tile_ref, basis_ref = refs
    total = stiff_ref[...]
    for d, other in enumerate(others):
        total = total + times_ref[d].astype(F32) * other[...]
    weight = stiff_ref[...] / total
    subs = schur_ref.shape[0]
    rows = lax.broadcasted_iota(jnp.int32, (NC, R), 0)
    for j in range(subs):
        hit = rows == primal_ref[j : j + 1, :]
        basis_ref[j] = jnp.where(hit, weight[j : j + 1, :], 0.0).astype(BF16)
        add_tile(half, j, off_ref, schur_ref, basis_ref, tile_ref)


def second_kernel(half, off_ref, schur_ref, basis_ref, tile_ref):
    for j in range(schur_ref.shape[0]):
        add_tile(half, j, off_ref, schur_ref, basis_ref, tile_ref)


def add_tile(half, j, off_ref, schur_ref, basis_ref, tile_ref):
    off = pl.multiple_of(off_ref[0], half)
    part = basis_ref[j, pl.ds(off, half), :]
    image = lax.dot_general(
        schur_ref[j], part, (((1,), (1,)), ((), ())), preferred_element_type=F32
    ).astype(BF16)
    term = jnp.dot(basis_ref[j], image, preferred_element_type=F32)
    if j == 0:
        tile_ref[...] = term
    else:
        tile_ref[...] += term


def split_kernel(rows, me_ref, own_ref, other_ref, *outs):
    for d, out in enumerate(outs):
        at = pl.ds(pl.multiple_of((me_ref[0] ^ d) * rows, rows), rows)
        out[...] = own_ref[at, :] + other_ref[at, :]


def sum_kernel(*refs):
    *pieces, out = refs
    total = pieces[0][...]
    for piece in pieces[1:]:
        total = total + piece[...]
    out[...] = total


def scale_kernel(chips, rows, half, me_ref, *refs):
    own, other = refs[:chips], refs[chips : 2 * chips]
    out_ref, tile, sems = refs[2 * chips :]
    chip, core = me_ref[0], me_ref[1]
    for pieces, column in ((own, core), (other, 1 - core)):
        for d, piece in enumerate(pieces):
            at = pl.ds(pl.multiple_of((chip ^ d) * rows, rows), rows)
            tile[at, pl.ds(pl.multiple_of(column * half, half), half)] = piece[...]
    mean = jnp.sum(jnp.abs(tile[...]), axis=1, keepdims=True) / NC
    scale = 1.0 / jnp.sqrt(mean + 1e-06)
    across = jnp.broadcast_to(scale, (NC, BLK)).T[:1, :]

    def copy(b):
        at = pl.ds(b * BLK, BLK)
        return pltpu.make_async_copy(tile.at[at], out_ref.at[at], sems.at[b])

    for b in range(NC // BLK):
        at = slice(b * BLK, (b + 1) * BLK)
        tile[at, :] = tile[at, :] * scale[at, :] * across
        copy(b).start()
    for b in range(NC // BLK):
        copy(b).wait()


def per_device(columns, line, coupling, local_block, counts, primal, partner):
    chips, half, rows = line // 2, NC // 2, NC // (line // 2)
    coupling, local_block, counts, primal = coupling[0], local_block[0], counts[0], primal[0]
    subs = coupling.shape[0]
    column, place = lax.axis_index("gx"), lax.axis_index("gy")
    core, chip = place % 2, place // 2
    spot = jnp.stack([chip, core]).astype(jnp.int32)

    stiff = diagonal(local_block)
    others, times = [], []
    for d in range(1, columns):
        others.append(lax.ppermute(stiff, "gx", [(i, i ^ d) for i in range(columns)]))
        times.append(jnp.sum((partner[:, column] == (column ^ d)).astype(jnp.int32)))
    times = jnp.stack(times)

    schur = schur_blocks(counts, coupling, local_block)

    first, basis = pl.pallas_call(
        functools.partial(first_kernel, half),
        out_shape=(pltpu.VMEM((NC, half), F32), pltpu.VMEM((subs, NC, R), BF16)),
        in_specs=[SSPEC, SSPEC] + [VSPEC] * (columns + 2),
        out_specs=(VSPEC, VSPEC),
        compiler_params=params(),
        name="first_half",
    )(((1 - core) * half)[None], times, primal, *in_vmem(stiff, *others, schur))
    swap = [(i, i ^ 1) for i in range(line)]
    other_core = lax.ppermute(first, "gy", swap)
    second = pl.pallas_call(
        functools.partial(second_kernel, half),
        out_shape=pltpu.VMEM((NC, half), F32),
        in_specs=[SSPEC, VSPEC, VSPEC],
        out_specs=VSPEC,
        compiler_params=params(),
        name="second_half",
    )((core * half)[None], *in_vmem(schur, basis))

    pieces = pl.pallas_call(
        functools.partial(split_kernel, rows),
        out_shape=tuple(pltpu.VMEM((rows, half), F32) for _ in range(chips)),
        in_specs=[SSPEC, VSPEC, VSPEC],
        out_specs=(VSPEC,) * chips,
        compiler_params=params(),
        name="split",
    )(spot, *in_vmem(second, other_core))

    def hop(d):
        return [(i, i ^ (2 * d)) for i in range(line)]

    arrived = [lax.ppermute(pieces[d], "gy", hop(d)) for d in range(1, chips)]
    mine = pl.pallas_call(
        sum_kernel,
        out_shape=pltpu.VMEM((rows, half), F32),
        in_specs=[VSPEC] * chips,
        out_specs=VSPEC,
        compiler_params=params(),
        name="sum",
    )(*in_vmem(pieces[0], *arrived))
    own = [mine] + [lax.ppermute(mine, "gy", hop(d)) for d in range(1, chips)]
    other = [lax.ppermute(piece, "gy", swap) for piece in own]
    result = pl.pallas_call(
        functools.partial(scale_kernel, chips, rows, half),
        out_shape=jax.ShapeDtypeStruct((NC, NC), F32),
        in_specs=[SSPEC] + [VSPEC] * (2 * chips),
        out_specs=ASPEC,
        scratch_shapes=[pltpu.VMEM((NC, NC), F32), pltpu.SemaphoreType.DMA((NC // BLK,))],
        compiler_params=params(),
        name="scale",
    )(spot, *in_vmem(*own, *other))
    return result[None]


def solution(mesh):
    placed = (
        P("gx", "gy", None, None),
        P("gx", "gy", None, None),
        P("gx", "gy"),
        P("gx", "gy", None),
        P(),
    )
    body = functools.partial(per_device, mesh.shape["gx"], mesh.shape["gy"])
    return jax.shard_map(
        body, mesh=mesh, in_specs=placed, out_specs=P("gx", None, None), check_vma=False
    )
```

```python
import functools

import jax
import jax.numpy as jnp
from jax import lax
from jax.experimental import pallas as pl
from jax.experimental.pallas import tpu as pltpu
from jax.sharding import PartitionSpec as P

BLK = 128
NC = 512
ROUNDS = 3
R = 512
NI = 1024
RB = 4
VMEM_LIMIT = 24 << 20

F32 = jnp.float32
BF16 = jnp.bfloat16


def params():
    return pltpu.CompilerParams(vmem_limit_bytes=VMEM_LIMIT)


def in_vmem(*arrays):
    return [pltpu.with_memory_space_constraint(a, pltpu.VMEM) for a in arrays]


def in_hbm(*arrays):
    return [pltpu.with_memory_space_constraint(a, pltpu.HBM) for a in arrays]


VSPEC = pl.BlockSpec(memory_space=pltpu.VMEM)
SSPEC = pl.BlockSpec(memory_space=pltpu.SMEM)
ASPEC = pl.BlockSpec(memory_space=pl.ANY)


def diag_kernel(block_ref, stiff_ref, held, sems):
    def copy(b):
        part = pl.ds(b * BLK, BLK)
        return pltpu.make_async_copy(block_ref.at[:, part, part], held.at[b], sems.at[b])

    for b in range(RB):
        copy(b).start()
    shape = (BLK, BLK)
    on = lax.broadcasted_iota(jnp.int32, shape, 0) == lax.broadcasted_iota(jnp.int32, shape, 1)
    for b in range(RB):
        copy(b).wait()
        tile = held[b].astype(F32)
        stiff_ref[:, b * BLK : (b + 1) * BLK] = jnp.sum(jnp.where(on[None], tile, 0.0), axis=1)


def diagonal(local_block):
    subs = local_block.shape[0]
    return pl.pallas_call(
        diag_kernel,
        out_shape=pltpu.VMEM((subs, R), F32),
        in_specs=[ASPEC],
        out_specs=VSPEC,
        scratch_shapes=[pltpu.VMEM((RB, subs, BLK, BLK), BF16), pltpu.SemaphoreType.DMA((RB,))],
        compiler_params=params(),
        name="diag",
    )(*in_hbm(local_block))


def schur_kernel(counts_ref, coupling_ref, block_ref, schur_ref):
    j = pl.program_id(0)
    for live in range(1, RB + 1):

        @pl.when(counts_ref[j] == live)
        def _():
            n = live * BLK
            c = coupling_ref[0, :, :n]
            gram = lax.dot_general(c, c, (((0,), (0,)), ((), ())), preferred_element_type=F32)
            schur_ref[0, :n, :n] = (block_ref[0, :n, :n].astype(F32) - gram).astype(BF16)
            if n < R:
                schur_ref[0, :n, n:] = jnp.zeros((n, R - n), BF16)
                schur_ref[0, n:, :] = jnp.zeros((R - n, R), BF16)


def schur_blocks(counts, coupling, local_block):
    subs = local_block.shape[0]
    return pl.pallas_call(
        schur_kernel,
        grid_spec=pltpu.PrefetchScalarGridSpec(
            num_scalar_prefetch=1,
            grid=(subs,),
            in_specs=[
                pl.BlockSpec((1, NI, R), lambda j, c: (j, 0, 0)),
                pl.BlockSpec((1, R, R), lambda j, c: (j, 0, 0)),
            ],
            out_specs=pl.BlockSpec((1, R, R), lambda j, c: (j, 0, 0)),
        ),
        out_shape=pltpu.VMEM((subs, R, R), BF16),
        compiler_params=params(),
        name="schur",
    )(counts, *in_hbm(coupling, local_block))


def place():
    at = lax.axis_index("gy")
    return lax.shift_right_logical(at, 1), at & 1


def first_kernel(half, partner_ref, primal_ref, stiff_ref, *refs):
    *others, schur_ref, tile_ref, basis_ref = refs
    column = lax.axis_index("gx")
    off = (1 - place()[1]) * half
    total = stiff_ref[...]
    for d, other in enumerate(others):
        times = jnp.int32(0)
        for r in range(ROUNDS):
            times += (partner_ref[r, column] == (column ^ (d + 1))).astype(jnp.int32)
        total = total + times.astype(F32) * other[...]
    weight = stiff_ref[...] / total
    subs = schur_ref.shape[0]
    rows = lax.broadcasted_iota(jnp.int32, (NC, R), 0)
    for j in range(subs):
        hit = rows == primal_ref[j : j + 1, :]
        basis_ref[j] = jnp.where(hit, weight[j : j + 1, :], 0.0).astype(BF16)
        add_tile(half, j, off, schur_ref, basis_ref, tile_ref)


def second_kernel(half, schur_ref, basis_ref, tile_ref):
    off = place()[1] * half
    for j in range(schur_ref.shape[0]):
        add_tile(half, j, off, schur_ref, basis_ref, tile_ref)


def add_tile(half, j, off, schur_ref, basis_ref, tile_ref):
    part = basis_ref[j, pl.ds(pl.multiple_of(off, half), half), :]
    image = lax.dot_general(
        schur_ref[j], part, (((1,), (1,)), ((), ())), preferred_element_type=F32
    ).astype(BF16)
    term = jnp.dot(basis_ref[j], image, preferred_element_type=F32)
    if j == 0:
        tile_ref[...] = term
    else:
        tile_ref[...] += term


def split_kernel(rows, own_ref, other_ref, *outs):
    chip = place()[0]
    for d, out in enumerate(outs):
        at = pl.ds(pl.multiple_of((chip ^ d) * rows, rows), rows)
        out[...] = own_ref[at, :] + other_ref[at, :]


def sum_kernel(*refs):
    *pieces, out = refs
    total = pieces[0][...]
    for piece in pieces[1:]:
        total = total + piece[...]
    out[...] = total


def scale_kernel(chips, rows, half, *refs):
    own, other = refs[:chips], refs[chips : 2 * chips]
    out_ref, tile, sems = refs[2 * chips :]
    chip, core = place()
    for pieces, column in ((own, core), (other, 1 - core)):
        for d, piece in enumerate(pieces):
            at = pl.ds(pl.multiple_of((chip ^ d) * rows, rows), rows)
            tile[at, pl.ds(pl.multiple_of(column * half, half), half)] = piece[...]
    mean = jnp.sum(jnp.abs(tile[...]), axis=1, keepdims=True) / NC
    scale = 1.0 / jnp.sqrt(mean + 1e-06)
    across = jnp.broadcast_to(scale, (NC, BLK)).T[:1, :]

    def copy(b):
        at = pl.ds(b * BLK, BLK)
        return pltpu.make_async_copy(tile.at[at], out_ref.at[at], sems.at[b])

    for b in range(NC // BLK):
        at = slice(b * BLK, (b + 1) * BLK)
        tile[at, :] = tile[at, :] * scale[at, :] * across
        copy(b).start()
    for b in range(NC // BLK):
        copy(b).wait()


def per_device(columns, line, coupling, local_block, counts, primal, partner):
    chips, half, rows = line // 2, NC // 2, NC // (line // 2)
    coupling, local_block, counts, primal = coupling[0], local_block[0], counts[0], primal[0]
    subs = coupling.shape[0]
    stiff = diagonal(local_block)
    others = [
        lax.ppermute(stiff, "gx", [(i, i ^ d) for i in range(columns)]) for d in range(1, columns)
    ]

    schur = schur_blocks(counts, coupling, local_block)

    first, basis = pl.pallas_call(
        functools.partial(first_kernel, half),
        out_shape=(pltpu.VMEM((NC, half), F32), pltpu.VMEM((subs, NC, R), BF16)),
        in_specs=[SSPEC] + [VSPEC] * (columns + 2),
        out_specs=(VSPEC, VSPEC),
        compiler_params=params(),
        name="first_half",
    )(partner, primal, *in_vmem(stiff, *others, schur))
    swap = [(i, i ^ 1) for i in range(line)]
    other_core = lax.ppermute(first, "gy", swap)
    second = pl.pallas_call(
        functools.partial(second_kernel, half),
        out_shape=pltpu.VMEM((NC, half), F32),
        in_specs=[VSPEC, VSPEC],
        out_specs=VSPEC,
        compiler_params=params(),
        name="second_half",
    )(*in_vmem(schur, basis))

    pieces = pl.pallas_call(
        functools.partial(split_kernel, rows),
        out_shape=tuple(pltpu.VMEM((rows, half), F32) for _ in range(chips)),
        in_specs=[VSPEC, VSPEC],
        out_specs=(VSPEC,) * chips,
        compiler_params=params(),
        name="split",
    )(*in_vmem(second, other_core))

    def hop(d):
        return [(i, i ^ (2 * d)) for i in range(line)]

    arrived = [lax.ppermute(pieces[d], "gy", hop(d)) for d in range(1, chips)]
    mine = pl.pallas_call(
        sum_kernel,
        out_shape=pltpu.VMEM((rows, half), F32),
        in_specs=[VSPEC] * chips,
        out_specs=VSPEC,
        compiler_params=params(),
        name="sum",
    )(*in_vmem(pieces[0], *arrived))
    own = [mine] + [lax.ppermute(mine, "gy", hop(d)) for d in range(1, chips)]
    other = [lax.ppermute(piece, "gy", swap) for piece in own]
    result = pl.pallas_call(
        functools.partial(scale_kernel, chips, rows, half),
        out_shape=jax.ShapeDtypeStruct((NC, NC), F32),
        in_specs=[VSPEC] * (2 * chips),
        out_specs=ASPEC,
        scratch_shapes=[pltpu.VMEM((NC, NC), F32), pltpu.SemaphoreType.DMA((NC // BLK,))],
        compiler_params=params(),
        name="scale",
    )(*in_vmem(*own, *other))
    return result[None]


def solution(mesh):
    placed = (
        P("gx", "gy", None, None),
        P("gx", "gy", None, None),
        P("gx", "gy"),
        P("gx", "gy", None),
        P(),
    )
    body = functools.partial(per_device, mesh.shape["gx"], mesh.shape["gy"])
    return jax.shard_map(
        body, mesh=mesh, in_specs=placed, out_specs=P("gx", None, None), check_vma=False
    )
```

```python
import functools

import jax
import jax.numpy as jnp
from jax import lax
from jax.experimental import pallas as pl
from jax.experimental.pallas import tpu as pltpu
from jax.sharding import PartitionSpec as P

BLK = 128
NC = 512
ROUNDS = 3
R = 512
NI = 1024
RB = 4
HEAD = 1
VMEM_LIMIT = 24 << 20

F32 = jnp.float32
BF16 = jnp.bfloat16


def params():
    return pltpu.CompilerParams(vmem_limit_bytes=VMEM_LIMIT)


def in_vmem(*arrays):
    return [pltpu.with_memory_space_constraint(a, pltpu.VMEM) for a in arrays]


def in_hbm(*arrays):
    return [pltpu.with_memory_space_constraint(a, pltpu.HBM) for a in arrays]


VSPEC = pl.BlockSpec(memory_space=pltpu.VMEM)
SSPEC = pl.BlockSpec(memory_space=pltpu.SMEM)
ASPEC = pl.BlockSpec(memory_space=pl.ANY)


def diag_kernel(block_ref, coupling_ref, stiff_ref, head_ref, held, sems, head_sems):
    def copy(b):
        part = pl.ds(b * BLK, BLK)
        return pltpu.make_async_copy(block_ref.at[:, part, part], held.at[b], sems.at[b])

    def head(j):
        return pltpu.make_async_copy(coupling_ref.at[j], head_ref.at[j], head_sems.at[j])

    for b in range(RB):
        copy(b).start()
    for j in range(HEAD):
        head(j).start()
    shape = (BLK, BLK)
    on = lax.broadcasted_iota(jnp.int32, shape, 0) == lax.broadcasted_iota(jnp.int32, shape, 1)
    for b in range(RB):
        copy(b).wait()
        tile = held[b].astype(F32)
        stiff_ref[:, b * BLK : (b + 1) * BLK] = jnp.sum(jnp.where(on[None], tile, 0.0), axis=1)
    for j in range(HEAD):
        head(j).wait()


def diagonal(local_block, coupling):
    subs = local_block.shape[0]
    return pl.pallas_call(
        diag_kernel,
        out_shape=(pltpu.VMEM((subs, R), F32), pltpu.VMEM((HEAD, NI, R), BF16)),
        in_specs=[ASPEC, ASPEC],
        out_specs=(VSPEC, VSPEC),
        scratch_shapes=[
            pltpu.VMEM((RB, subs, BLK, BLK), BF16),
            pltpu.SemaphoreType.DMA((RB,)),
            pltpu.SemaphoreType.DMA((HEAD,)),
        ],
        compiler_params=params(),
        name="diag",
    )(*in_hbm(local_block, coupling))


def schur_block(n, c, block, schur):
    at = 0
    while at < n:
        stop = min(n, at + 2 * BLK)
        here, rest = slice(at, stop), slice(stop, n)
        gram = lax.dot_general(
            c[:, here], c[:, here], (((0,), (0,)), ((), ())), preferred_element_type=F32
        )
        schur[here, here] = (block[here, here].astype(F32) - gram).astype(BF16)
        if stop < n:
            gram = lax.dot_general(
                c[:, here], c[:, rest], (((0,), (0,)), ((), ())), preferred_element_type=F32
            )
            schur[here, rest] = (block[here, rest].astype(F32) - gram).astype(BF16)
            schur[rest, here] = (block[rest, here].astype(F32) - gram.T).astype(BF16)
        at = stop
    if n < R:
        schur[:n, n:] = jnp.zeros((n, R - n), BF16)
        schur[n:, :] = jnp.zeros((R - n, R), BF16)


def schur_kernel(counts_ref, coupling_ref, head_ref, block_ref, schur_ref, held, sems):
    subs = block_ref.shape[0]

    def copy(j, n):
        part = pl.ds(0, n)
        return pltpu.make_async_copy(
            coupling_ref.at[j, :, part], held.at[j - HEAD, :, part], sems.at[j - HEAD]
        )

    def by_count(j, body):
        for live in range(1, RB + 1):
            pl.when(counts_ref[j] == live)(functools.partial(body, live * BLK))

    def send(j, _):
        by_count(j, lambda n: copy(j, n).start())
        return 0

    def from_head(j, _):
        by_count(j, lambda n: schur_block(n, head_ref.at[j], block_ref.at[j], schur_ref.at[j]))
        return 0

    def from_held(j, _):
        def body(n):
            copy(j, n).wait()
            schur_block(n, held.at[j - HEAD], block_ref.at[j], schur_ref.at[j])

        by_count(j, body)
        return 0

    lax.fori_loop(HEAD, subs, send, 0)
    lax.fori_loop(0, HEAD, from_head, 0)
    lax.fori_loop(HEAD, subs, from_held, 0)


def schur_blocks(counts, coupling, head, local_block):
    subs = local_block.shape[0]
    return pl.pallas_call(
        schur_kernel,
        out_shape=pltpu.VMEM((subs, R, R), BF16),
        in_specs=[SSPEC, ASPEC, VSPEC, VSPEC],
        out_specs=VSPEC,
        scratch_shapes=[
            pltpu.VMEM((subs - HEAD, NI, R), BF16),
            pltpu.SemaphoreType.DMA((subs - HEAD,)),
        ],
        compiler_params=params(),
        name="schur",
    )(counts, *in_hbm(coupling), *in_vmem(head, local_block))


def place():
    at = lax.axis_index("gy")
    return lax.shift_right_logical(at, 1), at & 1


def first_kernel(half, partner_ref, primal_ref, stiff_ref, *refs):
    *others, schur_ref, tile_ref, basis_ref = refs
    column = lax.axis_index("gx")
    off = (1 - place()[1]) * half
    total = stiff_ref[...]
    for d, other in enumerate(others):
        times = jnp.int32(0)
        for r in range(ROUNDS):
            times += (partner_ref[r, column] == (column ^ (d + 1))).astype(jnp.int32)
        total = total + times.astype(F32) * other[...]
    weight = (stiff_ref[...] / total).astype(BF16)
    rows = lax.broadcasted_iota(jnp.int32, (NC, R), 0).astype(jnp.int16)
    primal = primal_ref[...].astype(jnp.int16)
    for j in range(schur_ref.shape[0]):
        hit = rows == primal[j : j + 1, :]
        basis_ref[:, j * R : (j + 1) * R] = jnp.where(hit, weight[j : j + 1, :], jnp.zeros((), BF16))
    add_tiles(half, off, schur_ref, basis_ref, tile_ref)


def second_kernel(half, schur_ref, basis_ref, tile_ref):
    off = place()[1] * half
    add_tiles(half, off, schur_ref, basis_ref, tile_ref)


def add_tiles(half, off, schur_ref, basis_ref, tile_ref):
    images = []
    for j in range(schur_ref.shape[0]):
        part = basis_ref[pl.ds(pl.multiple_of(off, half), half), j * R : (j + 1) * R]
        images.append(lax.dot_general(
            schur_ref[j], part, (((1,), (1,)), ((), ())), preferred_element_type=F32
        ).astype(BF16))
    tile_ref[...] = jnp.dot(basis_ref[...], jnp.concatenate(images, axis=0), preferred_element_type=F32)


def split_kernel(rows, own_ref, other_ref, *outs):
    chip = place()[0]
    for d, out in enumerate(outs):
        at = pl.ds(pl.multiple_of((chip ^ d) * rows, rows), rows)
        out[...] = own_ref[at, :] + other_ref[at, :]


def sum_kernel(*refs):
    *pieces, out = refs
    total = pieces[0][...]
    for piece in pieces[1:]:
        total = total + piece[...]
    out[...] = total


def scale_kernel(chips, rows, half, *refs):
    own, other = refs[:chips], refs[chips : 2 * chips]
    out_ref, tile, sems = refs[2 * chips :]
    chip, core = place()
    for pieces, column in ((own, core), (other, 1 - core)):
        for d, piece in enumerate(pieces):
            at = pl.ds(pl.multiple_of((chip ^ d) * rows, rows), rows)
            tile[at, pl.ds(pl.multiple_of(column * half, half), half)] = piece[...]
    mean = jnp.sum(jnp.abs(tile[...]), axis=1, keepdims=True) / NC
    scale = 1.0 / jnp.sqrt(mean + 1e-06)
    across = jnp.broadcast_to(scale, (NC, BLK)).T[:1, :]

    def copy(b):
        at = pl.ds(b * BLK, BLK)
        return pltpu.make_async_copy(tile.at[at], out_ref.at[at], sems.at[b])

    for b in range(NC // BLK):
        at = slice(b * BLK, (b + 1) * BLK)
        tile[at, :] = tile[at, :] * scale[at, :] * across
        copy(b).start()
    for b in range(NC // BLK):
        copy(b).wait()


def per_device(columns, line, coupling, local_block, counts, primal, partner):
    chips, half, rows = line // 2, NC // 2, NC // (line // 2)
    coupling, local_block, counts, primal = coupling[0], local_block[0], counts[0], primal[0]
    subs = coupling.shape[0]
    stiff, head = diagonal(local_block, coupling)
    others = [
        lax.ppermute(stiff, "gx", [(i, i ^ d) for i in range(columns)]) for d in range(1, columns)
    ]

    schur = schur_blocks(counts, coupling, head, local_block)

    first, basis = pl.pallas_call(
        functools.partial(first_kernel, half),
        out_shape=(pltpu.VMEM((NC, half), F32), pltpu.VMEM((NC, subs * R), BF16)),
        in_specs=[SSPEC] + [VSPEC] * (columns + 2),
        out_specs=(VSPEC, VSPEC),
        compiler_params=params(),
        name="first_half",
    )(partner, primal, *in_vmem(stiff, *others, schur))
    swap = [(i, i ^ 1) for i in range(line)]
    other_core = lax.ppermute(first, "gy", swap)
    second = pl.pallas_call(
        functools.partial(second_kernel, half),
        out_shape=pltpu.VMEM((NC, half), F32),
        in_specs=[VSPEC, VSPEC],
        out_specs=VSPEC,
        compiler_params=params(),
        name="second_half",
    )(*in_vmem(schur, basis))

    pieces = pl.pallas_call(
        functools.partial(split_kernel, rows),
        out_shape=tuple(pltpu.VMEM((rows, half), F32) for _ in range(chips)),
        in_specs=[VSPEC, VSPEC],
        out_specs=(VSPEC,) * chips,
        compiler_params=params(),
        name="split",
    )(*in_vmem(second, other_core))

    def hop(d):
        return [(i, i ^ (2 * d)) for i in range(line)]

    arrived = [lax.ppermute(pieces[d], "gy", hop(d)) for d in range(1, chips)]
    mine = pl.pallas_call(
        sum_kernel,
        out_shape=pltpu.VMEM((rows, half), F32),
        in_specs=[VSPEC] * chips,
        out_specs=VSPEC,
        compiler_params=params(),
        name="sum",
    )(*in_vmem(pieces[0], *arrived))
    own = [mine] + [lax.ppermute(mine, "gy", hop(d)) for d in range(1, chips)]
    other = [lax.ppermute(piece, "gy", swap) for piece in own]
    result = pl.pallas_call(
        functools.partial(scale_kernel, chips, rows, half),
        out_shape=jax.ShapeDtypeStruct((NC, NC), F32),
        in_specs=[VSPEC] * (2 * chips),
        out_specs=ASPEC,
        scratch_shapes=[pltpu.VMEM((NC, NC), F32), pltpu.SemaphoreType.DMA((NC // BLK,))],
        compiler_params=params(),
        name="scale",
    )(*in_vmem(*own, *other))
    return result[None]


def solution(mesh):
    placed = (
        P("gx", "gy", None, None),
        P("gx", "gy", None, None),
        P("gx", "gy"),
        P("gx", "gy", None),
        P(),
    )
    body = functools.partial(per_device, mesh.shape["gx"], mesh.shape["gy"])
    return jax.shard_map(
        body, mesh=mesh, in_specs=placed, out_specs=P("gx", None, None), check_vma=False
    )
```

```python
import functools

import jax
import jax.numpy as jnp
from jax import lax
from jax.experimental import pallas as pl
from jax.experimental.pallas import tpu as pltpu
from jax.sharding import PartitionSpec as P

BLK = 128
NC = 512
ROUNDS = 3
R = 512
NI = 1024
RB = 4
HEAD = 2
HALF = NC // 2
PIECE = 128
VMEM_LIMIT = 24 << 20

F32 = jnp.float32
BF16 = jnp.bfloat16


def in_vmem(*arrays):
    return [pltpu.with_memory_space_constraint(a, pltpu.VMEM) for a in arrays]


def in_hbm(*arrays):
    return [pltpu.with_memory_space_constraint(a, pltpu.HBM) for a in arrays]


VSPEC = pl.BlockSpec(memory_space=pltpu.VMEM)
SSPEC = pl.BlockSpec(memory_space=pltpu.SMEM)
ASPEC = pl.BlockSpec(memory_space=pl.ANY)


def call(name, kernel, outs, in_specs, scratch=(), aliases={}):
    shapes = tuple(pltpu.VMEM(shape, dtype) for shape, dtype in outs)
    return pl.pallas_call(
        kernel,
        out_shape=shapes,
        in_specs=in_specs,
        out_specs=(VSPEC,) * len(shapes),
        scratch_shapes=list(scratch),
        input_output_aliases=aliases,
        compiler_params=pltpu.CompilerParams(vmem_limit_bytes=VMEM_LIMIT),
        name=name,
    )


def diag_kernel(block_ref, coupling_ref, stiff_ref, coupled_ref, held, sems, head_sems):
    def copy(b):
        part = pl.ds(b * BLK, BLK)
        return pltpu.make_async_copy(block_ref.at[:, part, part], held.at[b], sems.at[b])

    def head(j):
        return pltpu.make_async_copy(coupling_ref.at[j], coupled_ref.at[j], head_sems.at[j])

    for b in range(RB):
        copy(b).start()
    for j in range(HEAD):
        head(j).start()
    shape = (BLK, BLK)
    on = lax.broadcasted_iota(jnp.int32, shape, 0) == lax.broadcasted_iota(jnp.int32, shape, 1)
    for b in range(RB):
        copy(b).wait()
        tile = held[b].astype(F32)
        stiff_ref[:, b * BLK : (b + 1) * BLK] = jnp.sum(jnp.where(on[None], tile, 0.0), axis=1)
    for j in range(HEAD):
        head(j).wait()


def put(live, gram, block, schur, row, col):
    for r in range(0, gram.shape[0], BLK):
        for q in range(0, gram.shape[1], BLK):
            at = slice(row + r, row + r + BLK), slice(col + q, col + q + BLK)
            value = block[at].astype(F32) - gram[r : r + BLK, q : q + BLK]
            last = max(row + r, col + q) // BLK
            if last > 0:
                value = jnp.where(live > last, value, 0.0)
            schur[at] = value.astype(BF16)


def schur_block(live, c, block, schur):
    half = R // 2
    a, b = c[:, :half], c[:, half:]
    dims = (((0,), (0,)), ((), ()))
    gram = lax.dot_general(a, a, dims, preferred_element_type=F32)
    put(live, gram, block, schur, 0, 0)
    gram = lax.dot_general(a, b, dims, preferred_element_type=F32)
    put(live, gram, block, schur, 0, half)
    put(live, gram.T, block, schur, half, 0)
    gram = lax.dot_general(b, b, dims, preferred_element_type=F32)
    put(live, gram, block, schur, half, half)


def schur_kernel(first, last, here, stop, counts_ref, coupling_ref, _, block_ref, schur_ref, coupled_ref, sems):
    def copy(j):
        return pltpu.make_async_copy(coupling_ref.at[j], coupled_ref.at[j], sems.at[j - here])

    def start(j, carry):
        copy(j).start()
        return carry

    def wait(j, carry):
        copy(j).wait()
        return carry

    def pair(p, carry):
        j = first + 2 * p
        if last > here:
            @pl.when(j >= here)
            def _():
                copy(j).wait()
                copy(j + 1).wait()

        for k in range(2):
            schur_block(counts_ref[j + k], coupled_ref.at[j + k], block_ref.at[j + k], schur_ref.at[j + k - first])
        return carry

    lax.fori_loop(here, stop, start, 0)
    lax.fori_loop(0, (last - first) // 2, pair, 0)
    lax.fori_loop(max(here, last), stop, wait, 0)


def core():
    return lax.axis_index("gy") & 1


def first_kernel(partner_ref, primal_ref, stiff_ref, *refs):
    *others, schur_ref, up_ref, down_ref, basis_ref = refs
    subs = schur_ref.shape[0]
    column = lax.axis_index("gx")
    mine = stiff_ref[...]
    total = mine
    for d, other in enumerate(others, 1):
        times = jnp.int32(0)
        for r in range(ROUNDS):
            times += (partner_ref[r, column] == (column ^ d)).astype(jnp.int32)
        total = total + times.astype(F32) * other[...]
    weight = (mine / total).astype(BF16)
    primal = primal_ref[...]
    rows = lax.broadcasted_iota(jnp.int32, (NC, R), 0).astype(jnp.int16)
    part_rows = rows[:HALF]
    local = (primal - (1 - core()) * HALF).astype(jnp.int16)
    primal = primal.astype(jnp.int16)
    none = jnp.zeros((), BF16)
    images = []
    for j in range(subs):
        one = slice(j, j + 1)
        basis_ref[:, j * R : (j + 1) * R] = jnp.where(rows == primal[one], weight[one], none)
        part = jnp.where(part_rows == local[one], weight[one], none)
        images.append(image_of(schur_ref[j], part))
    image = jnp.concatenate(images, axis=0)
    for at, out_ref in ((0, up_ref), (HALF, down_ref)):
        out_ref[...] = jnp.dot(basis_ref[at : at + HALF], image, preferred_element_type=F32)


def image_of(schur, part):
    return lax.dot_general(
        schur, part, (((1,), (1,)), ((), ())), preferred_element_type=F32
    ).astype(BF16)


def upper_kernel(schur_ref, basis_ref, image_ref, up_ref):
    subs = schur_ref.shape[0]
    at = pl.ds(pl.multiple_of(core() * HALF, HALF), HALF)
    for j in range(subs):
        part = basis_ref[at, j * R : (j + 1) * R]
        image_ref[j * R : (j + 1) * R] = image_of(schur_ref[j], part)
    up_ref[...] = jnp.dot(basis_ref[:HALF], image_ref[...], preferred_element_type=F32)


def lower_kernel(basis_ref, image_ref, down_ref):
    down_ref[...] = jnp.dot(basis_ref[HALF:], image_ref[...], preferred_element_type=F32)


def pair_kernel(own_ref, other_ref, *outs):
    for d, out in enumerate(outs):
        at = slice(d * PIECE, (d + 1) * PIECE)
        out[...] = own_ref[at] + other_ref[at]


def add_kernel(own_ref, other_ref, out_ref):
    out_ref[...] = own_ref[...] + other_ref[...]


def scale_kernel(*refs):
    count = NC // PIECE
    own, other = refs[:count], refs[count : 2 * count]
    out_ref, tile, sems = refs[2 * count :]
    for pieces, column in ((own, core()), (other, 1 - core())):
        across = pl.ds(pl.multiple_of(column * HALF, HALF), HALF)
        for d, piece in enumerate(pieces):
            tile[d * PIECE : (d + 1) * PIECE, across] = piece[...]
    mean = jnp.sum(jnp.abs(tile[...]), axis=1, keepdims=True) / NC
    scale = 1.0 / jnp.sqrt(mean + 1e-06)
    across = jnp.broadcast_to(scale, (NC, BLK)).T[:1, :]

    def copy(b):
        at = pl.ds(b * BLK, BLK)
        return pltpu.make_async_copy(tile.at[at], out_ref.at[at], sems.at[b])

    for b in range(NC // BLK):
        at = slice(b * BLK, (b + 1) * BLK)
        tile[at, :] = tile[at, :] * scale[at, :] * across
        copy(b).start()
    for b in range(NC // BLK):
        copy(b).wait()


def per_device(columns, line, coupling, local_block, counts, primal, partner):
    coupling, local_block, counts, primal = coupling[0], local_block[0], counts[0], primal[0]
    subs = coupling.shape[0]
    coupled_shape = ((subs, NI, R), BF16)

    def swap(a, axis, size, bit):
        return lax.ppermute(a, axis, [(i, i ^ bit) for i in range(size)])

    stiff, coupled = call(
        "diag",
        diag_kernel,
        [((subs, R), F32), coupled_shape],
        [ASPEC, ASPEC],
        [
            pltpu.VMEM((RB, subs, BLK, BLK), BF16),
            pltpu.SemaphoreType.DMA((RB,)),
            pltpu.SemaphoreType.DMA((HEAD,)),
        ],
    )(*in_hbm(local_block, coupling))
    def schur(first, last, here, stop, coupled):
        return call(
            "schur",
            functools.partial(schur_kernel, first, last, here, stop),
            [((last - first, R, R), BF16), coupled_shape],
            [SSPEC, ASPEC, VSPEC, VSPEC],
            [pltpu.SemaphoreType.DMA((max(stop - here, 1),))],
            {2: 1},
        )(counts, *in_hbm(coupling), *in_vmem(coupled, local_block))

    others = [swap(stiff, "gx", columns, d) for d in range(1, columns)]
    schur_all, _ = schur(0, subs, HEAD, subs, coupled)

    block = ((HALF, HALF), F32)
    up, down, basis = call(
        "first_half", first_kernel, [block, block, ((NC, subs * R), BF16)], [SSPEC] + [VSPEC] * (columns + 2)
    )(partner, primal, *in_vmem(stiff, *others, schur_all))
    other_up, other_down = swap(up, "gy", line, 1), swap(down, "gy", line, 1)
    image, up = call(
        "upper", upper_kernel, [((subs * R, HALF), BF16), block], [VSPEC] * 2
    )(*in_vmem(schur_all, basis))
    pieces = ((PIECE, HALF), F32)
    pair = call("pair", pair_kernel, [pieces] * (HALF // PIECE), [VSPEC] * 2)
    upper = pair(*in_vmem(up, other_up))
    (down,) = call("lower", lower_kernel, [block], [VSPEC] * 2)(*in_vmem(basis, image))
    lower = pair(*in_vmem(down, other_down))

    add = call("add", add_kernel, [pieces], [VSPEC] * 2)
    steps = [2 << b for b in range((line // 2 - 1).bit_length())]
    own = [*upper, *lower]
    for step in range(len(steps)):
        for d in range(len(own)):
            bit = steps[step] if d % 2 == 0 else steps[-1 - step]
            (own[d],) = add(*in_vmem(own[d], swap(own[d], "gy", line, bit)))
    other = [swap(piece, "gy", line, 1) for piece in own]
    result = pl.pallas_call(
        scale_kernel,
        out_shape=jax.ShapeDtypeStruct((NC, NC), F32),
        in_specs=[VSPEC] * (2 * len(own)),
        out_specs=ASPEC,
        scratch_shapes=[pltpu.VMEM((NC, NC), F32), pltpu.SemaphoreType.DMA((NC // BLK,))],
        compiler_params=pltpu.CompilerParams(vmem_limit_bytes=VMEM_LIMIT),
        name="scale",
    )(*in_vmem(*own, *other))
    return result[None]


def solution(mesh):
    placed = (
        P("gx", "gy", None, None),
        P("gx", "gy", None, None),
        P("gx", "gy"),
        P("gx", "gy", None),
        P(),
    )
    body = functools.partial(per_device, mesh.shape["gx"], mesh.shape["gy"])
    return jax.shard_map(
        body, mesh=mesh, in_specs=placed, out_specs=P("gx", None, None), check_vma=False
    )
```

```python
import functools

import jax
import jax.numpy as jnp
from jax import lax
from jax.experimental import pallas as pl
from jax.experimental.pallas import tpu as pltpu
from jax.sharding import PartitionSpec as P

BLK = 128
NC = 512
ROUNDS = 3
R = 512
NI = 1024
RB = 4
HEAD = 2
HALF = NC // 2
PIECE = 128
VMEM_LIMIT = 24 << 20

F32 = jnp.float32
BF16 = jnp.bfloat16


def in_vmem(*arrays):
    return [pltpu.with_memory_space_constraint(a, pltpu.VMEM) for a in arrays]


def in_hbm(*arrays):
    return [pltpu.with_memory_space_constraint(a, pltpu.HBM) for a in arrays]


VSPEC = pl.BlockSpec(memory_space=pltpu.VMEM)
SSPEC = pl.BlockSpec(memory_space=pltpu.SMEM)
ASPEC = pl.BlockSpec(memory_space=pl.ANY)


def call(name, kernel, outs, in_specs, scratch=(), aliases={}):
    shapes = tuple(pltpu.VMEM(shape, dtype) for shape, dtype in outs)
    return pl.pallas_call(
        kernel,
        out_shape=shapes,
        in_specs=in_specs,
        out_specs=(VSPEC,) * len(shapes),
        scratch_shapes=list(scratch),
        input_output_aliases=aliases,
        compiler_params=pltpu.CompilerParams(vmem_limit_bytes=VMEM_LIMIT),
        name=name,
    )


def diag_kernel(block_ref, coupling_ref, stiff_ref, coupled_ref, held, sems, head_sems):
    def copy(b):
        part = pl.ds(b * BLK, BLK)
        return pltpu.make_async_copy(block_ref.at[:, part, part], held.at[b], sems.at[b])

    def head(j):
        return pltpu.make_async_copy(coupling_ref.at[j], coupled_ref.at[j], head_sems.at[j])

    for b in range(RB):
        copy(b).start()
    for j in range(HEAD):
        head(j).start()
    shape = (BLK, BLK)
    on = lax.broadcasted_iota(jnp.int32, shape, 0) == lax.broadcasted_iota(jnp.int32, shape, 1)
    for b in range(RB):
        copy(b).wait()
        tile = held[b].astype(F32)
        stiff_ref[:, b * BLK : (b + 1) * BLK] = jnp.sum(jnp.where(on[None], tile, 0.0), axis=1)
    for j in range(HEAD):
        head(j).wait()


def put(live, gram, block, schur, row, col):
    for r in range(0, gram.shape[0], BLK):
        for q in range(0, gram.shape[1], BLK):
            at = slice(row + r, row + r + BLK), slice(col + q, col + q + BLK)
            value = block[at].astype(F32) - gram[r : r + BLK, q : q + BLK]
            last = max(row + r, col + q) // BLK
            if last > 0:
                value = jnp.where(live > last, value, 0.0)
            schur[at] = value.astype(BF16)


def schur_block(live, c, block, schur):
    half = R // 2
    dims = (((0,), (0,)), ((), ()))
    gram = lax.dot_general(c[:, :half], c[...], dims, preferred_element_type=F32)
    put(live, gram, block, schur, 0, 0)
    put(live, gram[:, half:].T, block, schur, half, 0)
    gram = lax.dot_general(c[:, half:], c[:, half:], dims, preferred_element_type=F32)
    put(live, gram, block, schur, half, half)


def schur_kernel(first, last, here, stop, counts_ref, coupling_ref, _, block_ref, schur_ref, coupled_ref, sems):
    def copy(j):
        return pltpu.make_async_copy(coupling_ref.at[j], coupled_ref.at[j], sems.at[j - here])

    def start(j, carry):
        copy(j).start()
        return carry

    def wait(j, carry):
        copy(j).wait()
        return carry

    def pair(p, carry):
        j = first + 2 * p
        if last > here:
            @pl.when(j >= here)
            def _():
                copy(j).wait()
                copy(j + 1).wait()

        for k in range(2):
            schur_block(counts_ref[j + k], coupled_ref.at[j + k], block_ref.at[j + k], schur_ref.at[j + k - first])
        return carry

    lax.fori_loop(here, stop, start, 0)
    lax.fori_loop(0, (last - first) // 2, pair, 0)
    lax.fori_loop(max(here, last), stop, wait, 0)


def core():
    return lax.axis_index("gy") & 1


def first_kernel(partner_ref, primal_ref, stiff_ref, *refs):
    *others, schur_ref, tile_ref, basis_ref = refs
    subs = schur_ref.shape[0]
    column = lax.axis_index("gx")
    mine = stiff_ref[...]
    total = mine
    for d, other in enumerate(others, 1):
        times = jnp.int32(0)
        for r in range(ROUNDS):
            times += (partner_ref[r, column] == (column ^ d)).astype(jnp.int32)
        total = total + times.astype(F32) * other[...]
    weight = (mine / total).astype(BF16)
    primal = primal_ref[...]
    rows = lax.broadcasted_iota(jnp.int32, (NC, R), 0).astype(jnp.int16)
    part_rows = rows[:HALF]
    local = (primal - (1 - core()) * HALF).astype(jnp.int16)
    primal = primal.astype(jnp.int16)
    none = jnp.zeros((), BF16)
    images = []
    for j in range(subs):
        one = slice(j, j + 1)
        basis_ref[:, j * R : (j + 1) * R] = jnp.where(rows == primal[one], weight[one], none)
        part = jnp.where(part_rows == local[one], weight[one], none)
        images.append(image_of(schur_ref[j], part))
    image = jnp.concatenate(images, axis=0)
    for at in range(0, NC, 256):
        rows = slice(at, at + 256)
        tile_ref[rows] = jnp.dot(basis_ref[rows], image, preferred_element_type=F32)


def image_of(schur, part):
    return lax.dot_general(
        schur, part, (((1,), (1,)), ((), ())), preferred_element_type=F32
    ).astype(BF16)


def second_kernel(schur_ref, basis_ref, image_ref, up_ref):
    at = pl.ds(pl.multiple_of(core() * HALF, HALF), HALF)
    for j in range(schur_ref.shape[0]):
        part = basis_ref[at, j * R : (j + 1) * R]
        image_ref[j * R : (j + 1) * R] = image_of(schur_ref[j], part)
    up_ref[...] = jnp.dot(basis_ref[:HALF], image_ref[...], preferred_element_type=F32)


def pieces_kernel(basis_ref, image_ref, up_ref, other_ref, *outs):
    down = jnp.dot(basis_ref[HALF:], image_ref[...], preferred_element_type=F32)
    for d, out in enumerate(outs):
        at = slice(d * PIECE, (d + 1) * PIECE)
        if d * PIECE < HALF:
            out[...] = up_ref[at] + other_ref[at]
        else:
            out[...] = down[d * PIECE - HALF : (d + 1) * PIECE - HALF] + other_ref[at]


def add_kernel(own_ref, other_ref, out_ref):
    out_ref[...] = own_ref[...] + other_ref[...]


def scale_kernel(*refs):
    count = NC // PIECE
    own, other = refs[:count], refs[count : 2 * count]
    out_ref, tile, sems = refs[2 * count :]
    for pieces, column in ((own, core()), (other, 1 - core())):
        across = pl.ds(pl.multiple_of(column * HALF, HALF), HALF)
        for d, piece in enumerate(pieces):
            tile[d * PIECE : (d + 1) * PIECE, across] = piece[...]
    mean = jnp.sum(jnp.abs(tile[...]), axis=1, keepdims=True) / NC
    scale = 1.0 / jnp.sqrt(mean + 1e-06)
    across = jnp.broadcast_to(scale, (NC, BLK)).T[:1, :]

    def copy(b):
        at = pl.ds(b * BLK, BLK)
        return pltpu.make_async_copy(tile.at[at], out_ref.at[at], sems.at[b])

    for b in range(NC // BLK):
        at = slice(b * BLK, (b + 1) * BLK)
        tile[at, :] = tile[at, :] * scale[at, :] * across
        copy(b).start()
    for b in range(NC // BLK):
        copy(b).wait()


def per_device(columns, line, coupling, local_block, counts, primal, partner):
    coupling, local_block, counts, primal = coupling[0], local_block[0], counts[0], primal[0]
    subs = coupling.shape[0]
    coupled_shape = ((subs, NI, R), BF16)

    def swap(a, axis, size, bit):
        return lax.ppermute(a, axis, [(i, i ^ bit) for i in range(size)])

    stiff, coupled = call(
        "diag",
        diag_kernel,
        [((subs, R), F32), coupled_shape],
        [ASPEC, ASPEC],
        [
            pltpu.VMEM((RB, subs, BLK, BLK), BF16),
            pltpu.SemaphoreType.DMA((RB,)),
            pltpu.SemaphoreType.DMA((HEAD,)),
        ],
    )(*in_hbm(local_block, coupling))
    def schur(first, last, here, stop, coupled):
        return call(
            "schur",
            functools.partial(schur_kernel, first, last, here, stop),
            [((last - first, R, R), BF16), coupled_shape],
            [SSPEC, ASPEC, VSPEC, VSPEC],
            [pltpu.SemaphoreType.DMA((max(stop - here, 1),))],
            {2: 1},
        )(counts, *in_hbm(coupling), *in_vmem(coupled, local_block))

    others = [swap(stiff, "gx", columns, d) for d in range(1, columns)]
    schur_all, _ = schur(0, subs, HEAD, subs, coupled)

    half, pieces = ((NC, HALF), F32), ((PIECE, HALF), F32)
    tile, basis = call(
        "first", first_kernel, [half, ((NC, subs * R), BF16)], [SSPEC] + [VSPEC] * (columns + 2)
    )(partner, primal, *in_vmem(stiff, *others, schur_all))
    tile = swap(tile, "gy", line, 1)
    image, up = call(
        "second",
        second_kernel,
        [((subs * R, HALF), BF16), ((HALF, HALF), F32)],
        [VSPEC] * 2,
    )(*in_vmem(schur_all, basis))
    own = call("pieces", pieces_kernel, [pieces] * (NC // PIECE), [VSPEC] * 4)(
        *in_vmem(basis, image, up, tile)
    )
    own = list(own)

    add = call("add", add_kernel, [pieces], [VSPEC] * 2)
    steps = [2 << b for b in range((line // 2 - 1).bit_length())]
    for step in range(len(steps)):
        for d in range(len(own)):
            bit = steps[step] if d % 2 == 0 else steps[-1 - step]
            (own[d],) = add(*in_vmem(own[d], swap(own[d], "gy", line, bit)))
    other = [swap(piece, "gy", line, 1) for piece in own]
    result = pl.pallas_call(
        scale_kernel,
        out_shape=jax.ShapeDtypeStruct((NC, NC), F32),
        in_specs=[VSPEC] * (2 * len(own)),
        out_specs=ASPEC,
        scratch_shapes=[pltpu.VMEM((NC, NC), F32), pltpu.SemaphoreType.DMA((NC // BLK,))],
        compiler_params=pltpu.CompilerParams(vmem_limit_bytes=VMEM_LIMIT),
        name="scale",
    )(*in_vmem(*own, *other))
    return result[None]


def solution(mesh):
    placed = (
        P("gx", "gy", None, None),
        P("gx", "gy", None, None),
        P("gx", "gy"),
        P("gx", "gy", None),
        P(),
    )
    body = functools.partial(per_device, mesh.shape["gx"], mesh.shape["gy"])
    return jax.shard_map(
        body, mesh=mesh, in_specs=placed, out_specs=P("gx", None, None), check_vma=False
    )
```

```python
import functools

import jax
import jax.numpy as jnp
from jax import lax
from jax.experimental import pallas as pl
from jax.experimental.pallas import tpu as pltpu
from jax.sharding import PartitionSpec as P

BLK = 128
NC = 512
ROUNDS = 3
R = 512
NI = 1024
RB = 4
HEAD = 2
HALF = NC // 2
PIECE = 128
VMEM_LIMIT = 24 << 20

F32 = jnp.float32
BF16 = jnp.bfloat16


def in_vmem(*arrays):
    return [pltpu.with_memory_space_constraint(a, pltpu.VMEM) for a in arrays]


def in_hbm(*arrays):
    return [pltpu.with_memory_space_constraint(a, pltpu.HBM) for a in arrays]


VSPEC = pl.BlockSpec(memory_space=pltpu.VMEM)
SSPEC = pl.BlockSpec(memory_space=pltpu.SMEM)
ASPEC = pl.BlockSpec(memory_space=pl.ANY)


def call(name, kernel, outs, in_specs, scratch=(), aliases={}):
    shapes = tuple(pltpu.VMEM(shape, dtype) for shape, dtype in outs)
    return pl.pallas_call(
        kernel,
        out_shape=shapes,
        in_specs=in_specs,
        out_specs=(VSPEC,) * len(shapes),
        scratch_shapes=list(scratch),
        input_output_aliases=aliases,
        compiler_params=pltpu.CompilerParams(vmem_limit_bytes=VMEM_LIMIT),
        name=name,
    )


def diag_kernel(block_ref, coupling_ref, stiff_ref, coupled_ref, held, sems, head_sems):
    def copy(b):
        part = pl.ds(b * BLK, BLK)
        return pltpu.make_async_copy(block_ref.at[:, part, part], held.at[b], sems.at[b])

    def head(j):
        return pltpu.make_async_copy(coupling_ref.at[j], coupled_ref.at[j], head_sems.at[j])

    for b in range(RB):
        copy(b).start()
    for j in range(HEAD):
        head(j).start()
    shape = (BLK, BLK)
    on = lax.broadcasted_iota(jnp.int32, shape, 0) == lax.broadcasted_iota(jnp.int32, shape, 1)
    for b in range(RB):
        copy(b).wait()
        tile = held[b].astype(F32)
        stiff_ref[:, b * BLK : (b + 1) * BLK] = jnp.sum(jnp.where(on[None], tile, 0.0), axis=1)
    for j in range(HEAD):
        head(j).wait()


def put(live, gram, block, schur, row, col):
    for r in range(0, gram.shape[0], BLK):
        for q in range(0, gram.shape[1], BLK):
            at = slice(row + r, row + r + BLK), slice(col + q, col + q + BLK)
            value = block[at].astype(F32) - gram[r : r + BLK, q : q + BLK]
            last = max(row + r, col + q) // BLK
            if last > 0:
                value = jnp.where(live > last, value, 0.0)
            schur[at] = value.astype(BF16)


def schur_block(live, c, block, schur):
    half = R // 2
    dims = (((0,), (0,)), ((), ()))
    gram = lax.dot_general(c[:, :half], c[...], dims, preferred_element_type=F32)
    put(live, gram, block, schur, 0, 0)
    put(live, gram[:, half:].T, block, schur, half, 0)
    gram = lax.dot_general(c[:, half:], c[:, half:], dims, preferred_element_type=F32)
    put(live, gram, block, schur, half, half)


def schur_kernel(first, last, here, stop, counts_ref, coupling_ref, _, block_ref, schur_ref, coupled_ref, sems):
    def copy(j):
        return pltpu.make_async_copy(coupling_ref.at[j], coupled_ref.at[j], sems.at[j - here])

    def start(j, carry):
        copy(j).start()
        return carry

    def wait(j, carry):
        copy(j).wait()
        return carry

    def pair(p, carry):
        j = first + 2 * p
        if last > here:
            @pl.when(j >= here)
            def _():
                copy(j).wait()
                copy(j + 1).wait()

        for k in range(2):
            schur_block(counts_ref[j + k], coupled_ref.at[j + k], block_ref.at[j + k], schur_ref.at[j + k - first])
        return carry

    lax.fori_loop(here, stop, start, 0)
    lax.fori_loop(0, (last - first) // 2, pair, 0)
    lax.fori_loop(max(here, last), stop, wait, 0)


def core():
    return lax.axis_index("gy") & 1


def first_kernel(partner_ref, primal_ref, stiff_ref, *refs):
    *others, schur_ref, tile_ref, basis_ref = refs
    subs = schur_ref.shape[0]
    column = lax.axis_index("gx")
    mine = stiff_ref[...]
    total = mine
    for d, other in enumerate(others, 1):
        times = jnp.int32(0)
        for r in range(ROUNDS):
            times += (partner_ref[r, column] == (column ^ d)).astype(jnp.int32)
        total = total + times.astype(F32) * other[...]
    weight = (mine / total).astype(BF16)
    primal = primal_ref[...]
    rows = lax.broadcasted_iota(jnp.int32, (NC, R), 0).astype(jnp.int16)
    part_rows = rows[:HALF]
    local = (primal - (1 - core()) * HALF).astype(jnp.int16)
    primal = primal.astype(jnp.int16)
    none = jnp.zeros((), BF16)
    images = []
    for j in range(subs):
        one = slice(j, j + 1)
        basis_ref[:, j * R : (j + 1) * R] = jnp.where(rows == primal[one], weight[one], none)
        part = jnp.where(part_rows == local[one], weight[one], none)
        images.append(image_of(schur_ref[j], part))
    image = jnp.concatenate(images, axis=0)
    for at in range(0, NC, 256):
        rows = slice(at, at + 256)
        tile_ref[rows] = jnp.dot(basis_ref[rows], image, preferred_element_type=F32)


def image_of(schur, part):
    return lax.dot_general(
        schur, part, (((1,), (1,)), ((), ())), preferred_element_type=F32
    ).astype(BF16)


def second_kernel(schur_ref, basis_ref, image_ref, up_ref):
    at = pl.ds(pl.multiple_of(core() * HALF, HALF), HALF)
    for j in range(schur_ref.shape[0]):
        part = basis_ref[at, j * R : (j + 1) * R]
        image_ref[j * R : (j + 1) * R] = image_of(schur_ref[j], part)
    up_ref[...] = jnp.dot(basis_ref[:HALF], image_ref[...], preferred_element_type=F32)


def upper_kernel(own_ref, other_ref, token_ref, *outs):
    for d, out in enumerate(outs):
        at = slice(d * PIECE, (d + 1) * PIECE)
        out[...] = own_ref[at] + other_ref[at]
    token_ref[...] = outs[0][:8, :BLK]


def lower_kernel(basis_ref, image_ref, other_ref, _, *outs):
    down = jnp.dot(basis_ref[HALF:], image_ref[...], preferred_element_type=F32)
    for d, out in enumerate(outs):
        at = slice(d * PIECE, (d + 1) * PIECE)
        out[...] = down[at] + other_ref[HALF + d * PIECE : HALF + (d + 1) * PIECE]


def add_kernel(own_ref, other_ref, out_ref):
    out_ref[...] = own_ref[...] + other_ref[...]


def scale_kernel(*refs):
    count = NC // PIECE
    own, other = refs[:count], refs[count : 2 * count]
    out_ref, tile, sems = refs[2 * count :]

    def copy(d):
        at = pl.ds(d * PIECE, PIECE)
        return pltpu.make_async_copy(tile.at[at], out_ref.at[at], sems.at[d])

    down, across = [], []
    for d in range(count):
        total = jnp.abs(own[d][...]) + jnp.abs(other[d][...])
        mean = jnp.sum(total, axis=1, keepdims=True) / NC
        scale = jnp.broadcast_to(1.0 / jnp.sqrt(mean + 1e-06), (PIECE, BLK))
        down.append(scale[:, :1])
        across.append(scale.T[:1, :])
    halves = [jnp.concatenate(across[:2], axis=1), jnp.concatenate(across[2:], axis=1)]
    first = core() == 0
    mine = jnp.where(first, halves[0], halves[1])
    theirs = jnp.where(first, halves[1], halves[0])
    here = pl.ds(pl.multiple_of(core() * HALF, HALF), HALF)
    there = pl.ds(pl.multiple_of((1 - core()) * HALF, HALF), HALF)
    for d in range(count):
        at = slice(d * PIECE, (d + 1) * PIECE)
        tile[at, here] = own[d][...] * down[d] * mine
        tile[at, there] = other[d][...] * down[d] * theirs
        copy(d).start()
    for d in range(count):
        copy(d).wait()


def per_device(columns, line, coupling, local_block, counts, primal, partner):
    coupling, local_block, counts, primal = coupling[0], local_block[0], counts[0], primal[0]
    subs = coupling.shape[0]
    coupled_shape = ((subs, NI, R), BF16)

    def swap(a, axis, size, bit):
        return lax.ppermute(a, axis, [(i, i ^ bit) for i in range(size)])

    stiff, coupled = call(
        "diag",
        diag_kernel,
        [((subs, R), F32), coupled_shape],
        [ASPEC, ASPEC],
        [
            pltpu.VMEM((RB, subs, BLK, BLK), BF16),
            pltpu.SemaphoreType.DMA((RB,)),
            pltpu.SemaphoreType.DMA((HEAD,)),
        ],
    )(*in_hbm(local_block, coupling))
    def schur(first, last, here, stop, coupled):
        return call(
            "schur",
            functools.partial(schur_kernel, first, last, here, stop),
            [((last - first, R, R), BF16), coupled_shape],
            [SSPEC, ASPEC, VSPEC, VSPEC],
            [pltpu.SemaphoreType.DMA((max(stop - here, 1),))],
            {2: 1},
        )(counts, *in_hbm(coupling), *in_vmem(coupled, local_block))

    others = [swap(stiff, "gx", columns, d) for d in range(1, columns)]
    schur_all, _ = schur(0, subs, HEAD, subs, coupled)

    half, pieces = ((NC, HALF), F32), ((PIECE, HALF), F32)
    tile, basis = call(
        "first", first_kernel, [half, ((NC, subs * R), BF16)], [SSPEC] + [VSPEC] * (columns + 2)
    )(partner, primal, *in_vmem(stiff, *others, schur_all))
    tile = swap(tile, "gy", line, 1)
    image, up = call(
        "second",
        second_kernel,
        [((subs * R, HALF), BF16), ((HALF, HALF), F32)],
        [VSPEC] * 2,
    )(*in_vmem(schur_all, basis))
    count = HALF // PIECE
    token, *upper = call(
        "upper", upper_kernel, [((8, BLK), F32)] + [pieces] * count, [VSPEC] * 2
    )(*in_vmem(up, tile))
    token = swap(token, "gy", line, 1)
    lower = call("lower", lower_kernel, [pieces] * count, [VSPEC] * 4)(
        *in_vmem(basis, image, tile, token)
    )
    own = [*upper, *lower]

    add = call("add", add_kernel, [pieces], [VSPEC] * 2)
    steps = [2 << b for b in range((line // 2 - 1).bit_length())]
    for step in range(len(steps)):
        for d in range(len(own)):
            bit = steps[step] if d % 2 == 0 else steps[-1 - step]
            (own[d],) = add(*in_vmem(own[d], swap(own[d], "gy", line, bit)))
    other = [swap(piece, "gy", line, 1) for piece in own]
    result = pl.pallas_call(
        scale_kernel,
        out_shape=jax.ShapeDtypeStruct((NC, NC), F32),
        in_specs=[VSPEC] * (2 * len(own)),
        out_specs=ASPEC,
        scratch_shapes=[pltpu.VMEM((NC, NC), F32), pltpu.SemaphoreType.DMA((NC // BLK,))],
        compiler_params=pltpu.CompilerParams(vmem_limit_bytes=VMEM_LIMIT),
        name="scale",
    )(*in_vmem(*own, *other))
    return result[None]


def solution(mesh):
    placed = (
        P("gx", "gy", None, None),
        P("gx", "gy", None, None),
        P("gx", "gy"),
        P("gx", "gy", None),
        P(),
    )
    body = functools.partial(per_device, mesh.shape["gx"], mesh.shape["gy"])
    return jax.shard_map(
        body, mesh=mesh, in_specs=placed, out_specs=P("gx", None, None), check_vma=False
    )
```

```python
import functools

import jax
import jax.numpy as jnp
from jax import lax
from jax.experimental import pallas as pl
from jax.experimental.pallas import tpu as pltpu
from jax.sharding import PartitionSpec as P

BLK = 128
NC = 512
ROUNDS = 3
R = 512
NI = 1024
RB = 4
HEAD = 2
HALF = NC // 2
PIECE = 128
VMEM_LIMIT = 24 << 20

F32 = jnp.float32
BF16 = jnp.bfloat16


def in_vmem(*arrays):
    return [pltpu.with_memory_space_constraint(a, pltpu.VMEM) for a in arrays]


def in_hbm(*arrays):
    return [pltpu.with_memory_space_constraint(a, pltpu.HBM) for a in arrays]


VSPEC = pl.BlockSpec(memory_space=pltpu.VMEM)
SSPEC = pl.BlockSpec(memory_space=pltpu.SMEM)
ASPEC = pl.BlockSpec(memory_space=pl.ANY)


def call(name, kernel, outs, in_specs, scratch=(), aliases={}):
    shapes = tuple(pltpu.VMEM(shape, dtype) for shape, dtype in outs)
    return pl.pallas_call(
        kernel,
        out_shape=shapes,
        in_specs=in_specs,
        out_specs=(VSPEC,) * len(shapes),
        scratch_shapes=list(scratch),
        input_output_aliases=aliases,
        compiler_params=pltpu.CompilerParams(vmem_limit_bytes=VMEM_LIMIT),
        name=name,
    )


def diag_kernel(block_ref, coupling_ref, stiff_ref, coupled_ref, held, sems, head_sems):
    def copy(b):
        part = pl.ds(b * BLK, BLK)
        return pltpu.make_async_copy(block_ref.at[:, part, part], held.at[b], sems.at[b])

    def head(j):
        return pltpu.make_async_copy(coupling_ref.at[j], coupled_ref.at[j], head_sems.at[j])

    for b in range(RB):
        copy(b).start()
    for j in range(HEAD):
        head(j).start()
    shape = (BLK, BLK)
    on = lax.broadcasted_iota(jnp.int32, shape, 0) == lax.broadcasted_iota(jnp.int32, shape, 1)
    for b in range(RB):
        copy(b).wait()
        tile = held[b].astype(F32)
        stiff_ref[:, b * BLK : (b + 1) * BLK] = jnp.sum(jnp.where(on[None], tile, 0.0), axis=1)
    for j in range(HEAD):
        head(j).wait()


def put(live, gram, block, schur, row, col):
    for r in range(0, gram.shape[0], BLK):
        for q in range(0, gram.shape[1], BLK):
            at = slice(row + r, row + r + BLK), slice(col + q, col + q + BLK)
            value = block[at].astype(F32) - gram[r : r + BLK, q : q + BLK]
            last = max(row + r, col + q) // BLK
            if last > 0:
                value = jnp.where(live > last, value, 0.0)
            schur[at] = value.astype(BF16)


def schur_block(live, c, block, schur):
    half = R // 2
    dims = (((0,), (0,)), ((), ()))
    gram = lax.dot_general(c[:, :half], c[...], dims, preferred_element_type=F32)
    put(live, gram, block, schur, 0, 0)
    put(live, gram[:, half:].T, block, schur, half, 0)
    gram = lax.dot_general(c[:, half:], c[:, half:], dims, preferred_element_type=F32)
    put(live, gram, block, schur, half, half)


def schur_kernel(first, last, here, stop, counts_ref, coupling_ref, _, block_ref, schur_ref, coupled_ref, sems):
    def each(j, act):
        for live in range(1, RB + 1):

            @pl.when(counts_ref[j] == live)
            def _():
                part = pl.ds(0, live * BLK)
                act(
                    pltpu.make_async_copy(
                        coupling_ref.at[j, :, part], coupled_ref.at[j, :, part], sems.at[j - here]
                    )
                )

    def start(j, carry):
        each(j, lambda copy: copy.start())
        return carry

    def wait(j, carry):
        each(j, lambda copy: copy.wait())
        return carry

    def pair(p, carry):
        j = first + 2 * p
        if last > here:
            @pl.when(j >= here)
            def _():
                wait(j, 0)
                wait(j + 1, 0)

        for k in range(2):
            schur_block(counts_ref[j + k], coupled_ref.at[j + k], block_ref.at[j + k], schur_ref.at[j + k - first])
        return carry

    lax.fori_loop(here, stop, start, 0)
    lax.fori_loop(0, (last - first) // 2, pair, 0)
    lax.fori_loop(max(here, last), stop, wait, 0)


def core():
    return lax.axis_index("gy") & 1


def first_kernel(partner_ref, primal_ref, stiff_ref, *refs):
    *others, schur_ref, tile_ref, basis_ref = refs
    subs = schur_ref.shape[0]
    column = lax.axis_index("gx")
    mine = stiff_ref[...]
    total = mine
    for d, other in enumerate(others, 1):
        times = jnp.int32(0)
        for r in range(ROUNDS):
            times += (partner_ref[r, column] == (column ^ d)).astype(jnp.int32)
        total = total + times.astype(F32) * other[...]
    weight = (mine / total).astype(BF16)
    primal = primal_ref[...]
    rows = lax.broadcasted_iota(jnp.int32, (NC, R), 0).astype(jnp.int16)
    part_rows = rows[:HALF]
    local = (primal - (1 - core()) * HALF).astype(jnp.int16)
    primal = primal.astype(jnp.int16)
    none = jnp.zeros((), BF16)
    images = []
    for j in range(subs):
        one = slice(j, j + 1)
        basis_ref[:, j * R : (j + 1) * R] = jnp.where(rows == primal[one], weight[one], none)
        part = jnp.where(part_rows == local[one], weight[one], none)
        images.append(image_of(schur_ref[j], part))
    image = jnp.concatenate(images, axis=0)
    for at in range(0, NC, 256):
        rows = slice(at, at + 256)
        tile_ref[rows] = jnp.dot(basis_ref[rows], image, preferred_element_type=F32)


def image_of(schur, part):
    return lax.dot_general(
        schur, part, (((1,), (1,)), ((), ())), preferred_element_type=F32
    ).astype(BF16)


def second_kernel(schur_ref, basis_ref, image_ref, up_ref):
    at = pl.ds(pl.multiple_of(core() * HALF, HALF), HALF)
    for j in range(schur_ref.shape[0]):
        part = basis_ref[at, j * R : (j + 1) * R]
        image_ref[j * R : (j + 1) * R] = image_of(schur_ref[j], part)
    up_ref[...] = jnp.dot(basis_ref[:HALF], image_ref[...], preferred_element_type=F32)


def upper_kernel(own_ref, other_ref, token_ref, *outs):
    for d, out in enumerate(outs):
        at = slice(d * PIECE, (d + 1) * PIECE)
        out[...] = own_ref[at] + other_ref[at]
    token_ref[...] = outs[0][:8, :BLK]


def lower_kernel(basis_ref, image_ref, other_ref, _, *outs):
    down = jnp.dot(basis_ref[HALF:], image_ref[...], preferred_element_type=F32)
    for d, out in enumerate(outs):
        at = slice(d * PIECE, (d + 1) * PIECE)
        out[...] = down[at] + other_ref[HALF + d * PIECE : HALF + (d + 1) * PIECE]


def add_kernel(own_ref, other_ref, out_ref):
    out_ref[...] = own_ref[...] + other_ref[...]


def scale_kernel(*refs):
    count = NC // PIECE
    own, other = refs[:count], refs[count : 2 * count]
    out_ref, tile, sems = refs[2 * count :]

    def copy(d):
        at = pl.ds(d * PIECE, PIECE)
        return pltpu.make_async_copy(tile.at[at], out_ref.at[at], sems.at[d])

    down, across = [], []
    for d in range(count):
        total = jnp.abs(own[d][...]) + jnp.abs(other[d][...])
        mean = jnp.sum(total, axis=1, keepdims=True) / NC
        scale = jnp.broadcast_to(1.0 / jnp.sqrt(mean + 1e-06), (PIECE, BLK))
        down.append(scale[:, :1])
        across.append(scale.T[:1, :])
    halves = [jnp.concatenate(across[:2], axis=1), jnp.concatenate(across[2:], axis=1)]
    first = core() == 0
    mine = jnp.where(first, halves[0], halves[1])
    theirs = jnp.where(first, halves[1], halves[0])
    here = pl.ds(pl.multiple_of(core() * HALF, HALF), HALF)
    there = pl.ds(pl.multiple_of((1 - core()) * HALF, HALF), HALF)
    for d in range(count):
        at = slice(d * PIECE, (d + 1) * PIECE)
        tile[at, here] = own[d][...] * down[d] * mine
        tile[at, there] = other[d][...] * down[d] * theirs
        copy(d).start()
    for d in range(count):
        copy(d).wait()


def per_device(columns, line, coupling, local_block, counts, primal, partner):
    coupling, local_block, counts, primal = coupling[0], local_block[0], counts[0], primal[0]
    subs = coupling.shape[0]
    coupled_shape = ((subs, NI, R), BF16)

    def swap(a, axis, size, bit):
        return lax.ppermute(a, axis, [(i, i ^ bit) for i in range(size)])

    stiff, coupled = call(
        "diag",
        diag_kernel,
        [((subs, R), F32), coupled_shape],
        [ASPEC, ASPEC],
        [
            pltpu.VMEM((RB, subs, BLK, BLK), BF16),
            pltpu.SemaphoreType.DMA((RB,)),
            pltpu.SemaphoreType.DMA((HEAD,)),
        ],
    )(*in_hbm(local_block, coupling))
    def schur(first, last, here, stop, coupled):
        return call(
            "schur",
            functools.partial(schur_kernel, first, last, here, stop),
            [((last - first, R, R), BF16), coupled_shape],
            [SSPEC, ASPEC, VSPEC, VSPEC],
            [pltpu.SemaphoreType.DMA((max(stop - here, 1),))],
            {2: 1},
        )(counts, *in_hbm(coupling), *in_vmem(coupled, local_block))

    others = [swap(stiff, "gx", columns, d) for d in range(1, columns)]
    schur_all, _ = schur(0, subs, HEAD, subs, coupled)

    half, pieces = ((NC, HALF), F32), ((PIECE, HALF), F32)
    tile, basis = call(
        "first", first_kernel, [half, ((NC, subs * R), BF16)], [SSPEC] + [VSPEC] * (columns + 2)
    )(partner, primal, *in_vmem(stiff, *others, schur_all))
    tile = swap(tile, "gy", line, 1)
    image, up = call(
        "second",
        second_kernel,
        [((subs * R, HALF), BF16), ((HALF, HALF), F32)],
        [VSPEC] * 2,
    )(*in_vmem(schur_all, basis))
    count = HALF // PIECE
    token, *upper = call(
        "upper", upper_kernel, [((8, BLK), F32)] + [pieces] * count, [VSPEC] * 2
    )(*in_vmem(up, tile))
    token = swap(token, "gy", line, 1)
    lower = call("lower", lower_kernel, [pieces] * count, [VSPEC] * 4)(
        *in_vmem(basis, image, tile, token)
    )
    own = [*upper, *lower]

    add = call("add", add_kernel, [pieces], [VSPEC] * 2)
    steps = [2 << b for b in range((line // 2 - 1).bit_length())]
    for step in range(len(steps)):
        for d in range(len(own)):
            bit = steps[step] if d % 2 == 0 else steps[-1 - step]
            (own[d],) = add(*in_vmem(own[d], swap(own[d], "gy", line, bit)))
    other = [swap(piece, "gy", line, 1) for piece in own]
    result = pl.pallas_call(
        scale_kernel,
        out_shape=jax.ShapeDtypeStruct((NC, NC), F32),
        in_specs=[VSPEC] * (2 * len(own)),
        out_specs=ASPEC,
        scratch_shapes=[pltpu.VMEM((NC, NC), F32), pltpu.SemaphoreType.DMA((NC // BLK,))],
        compiler_params=pltpu.CompilerParams(vmem_limit_bytes=VMEM_LIMIT),
        name="scale",
    )(*in_vmem(*own, *other))
    return result[None]


def solution(mesh):
    placed = (
        P("gx", "gy", None, None),
        P("gx", "gy", None, None),
        P("gx", "gy"),
        P("gx", "gy", None),
        P(),
    )
    body = functools.partial(per_device, mesh.shape["gx"], mesh.shape["gy"])
    return jax.shard_map(
        body, mesh=mesh, in_specs=placed, out_specs=P("gx", None, None), check_vma=False
    )
```

```python
import functools

import jax
import jax.numpy as jnp
from jax import lax
from jax.experimental import pallas as pl
from jax.experimental.pallas import tpu as pltpu
from jax.sharding import PartitionSpec as P

BLK = 128
NC = 512
ROUNDS = 3
R = 512
NI = 1024
RB = 4
HEAD = 2
HALF = NC // 2
PIECE = 128
VMEM_LIMIT = 24 << 20

F32 = jnp.float32
BF16 = jnp.bfloat16


def in_vmem(*arrays):
    return [pltpu.with_memory_space_constraint(a, pltpu.VMEM) for a in arrays]


def in_hbm(*arrays):
    return [pltpu.with_memory_space_constraint(a, pltpu.HBM) for a in arrays]


VSPEC = pl.BlockSpec(memory_space=pltpu.VMEM)
SSPEC = pl.BlockSpec(memory_space=pltpu.SMEM)
ASPEC = pl.BlockSpec(memory_space=pl.ANY)


def call(name, kernel, outs, in_specs, scratch=(), aliases={}):
    shapes = tuple(pltpu.VMEM(shape, dtype) for shape, dtype in outs)
    return pl.pallas_call(
        kernel,
        out_shape=shapes,
        in_specs=in_specs,
        out_specs=(VSPEC,) * len(shapes),
        scratch_shapes=list(scratch),
        input_output_aliases=aliases,
        compiler_params=pltpu.CompilerParams(vmem_limit_bytes=VMEM_LIMIT),
        name=name,
    )


def diag_kernel(block_ref, coupling_ref, stiff_ref, coupled_ref, held, sems, head_sems):
    def copy(b):
        part = pl.ds(b * BLK, BLK)
        return pltpu.make_async_copy(block_ref.at[:, part, part], held.at[b], sems.at[b])

    def head(j):
        return pltpu.make_async_copy(coupling_ref.at[j], coupled_ref.at[j], head_sems.at[j])

    for b in range(RB):
        copy(b).start()
    for j in range(HEAD):
        head(j).start()
    shape = (BLK, BLK)
    on = lax.broadcasted_iota(jnp.int32, shape, 0) == lax.broadcasted_iota(jnp.int32, shape, 1)
    for b in range(RB):
        copy(b).wait()
        tile = held[b].astype(F32)
        stiff_ref[:, b * BLK : (b + 1) * BLK] = jnp.sum(jnp.where(on[None], tile, 0.0), axis=1)
    for j in range(HEAD):
        head(j).wait()


def put(live, gram, block, schur, row, col):
    for r in range(0, gram.shape[0], BLK):
        for q in range(0, gram.shape[1], BLK):
            at = slice(row + r, row + r + BLK), slice(col + q, col + q + BLK)
            value = block[at].astype(F32) - gram[r : r + BLK, q : q + BLK]
            last = max(row + r, col + q) // BLK
            if last > 0:
                value = jnp.where(live > last, value, 0.0)
            schur[at] = value.astype(BF16)


def schur_block(live, c, block, schur):
    half = R // 2
    dims = (((0,), (0,)), ((), ()))
    gram = lax.dot_general(c[:, :half], c[...], dims, preferred_element_type=F32)
    put(live, gram, block, schur, 0, 0)
    put(live, gram[:, half:].T, block, schur, half, 0)
    gram = lax.dot_general(c[:, half:], c[:, half:], dims, preferred_element_type=F32)
    put(live, gram, block, schur, half, half)


def schur_kernel(first, last, here, stop, counts_ref, coupling_ref, _, block_ref, schur_ref, coupled_ref, sems):
    def each(j, act):
        for live in range(1, RB + 1):

            @pl.when(counts_ref[j] == live)
            def _():
                part = pl.ds(0, live * BLK)
                act(
                    pltpu.make_async_copy(
                        coupling_ref.at[j, :, part], coupled_ref.at[j, :, part], sems.at[j - here]
                    )
                )

    def start(j, carry):
        each(j, lambda copy: copy.start())
        return carry

    def wait(j, carry):
        each(j, lambda copy: copy.wait())
        return carry

    def pair(p, carry):
        j = first + 2 * p
        if last > here:
            @pl.when(j >= here)
            def _():
                wait(j, 0)
                wait(j + 1, 0)

        for k in range(2):
            schur_block(counts_ref[j + k], coupled_ref.at[j + k], block_ref.at[j + k], schur_ref.at[j + k - first])
        return carry

    lax.fori_loop(here, stop, start, 0)
    lax.fori_loop(0, (last - first) // 2, pair, 0)
    lax.fori_loop(max(here, last), stop, wait, 0)


def core():
    return lax.axis_index("gy") & 1


def first_kernel(partner_ref, primal_ref, stiff_ref, *refs):
    *others, schur_ref, tile_ref, basis_ref = refs
    subs = schur_ref.shape[0]
    column = lax.axis_index("gx")
    mine = stiff_ref[...]
    total = mine
    for d, other in enumerate(others, 1):
        times = jnp.int32(0)
        for r in range(ROUNDS):
            times += (partner_ref[r, column] == (column ^ d)).astype(jnp.int32)
        total = total + times.astype(F32) * other[...]
    weight = (mine / total).astype(BF16)
    primal = primal_ref[...]
    rows = lax.broadcasted_iota(jnp.int32, (NC, R), 0).astype(jnp.int16)
    part_rows = rows[:HALF]
    local = (primal - (1 - core()) * HALF).astype(jnp.int16)
    primal = primal.astype(jnp.int16)
    none = jnp.zeros((), BF16)
    images = []
    for j in range(subs):
        one = slice(j, j + 1)
        basis_ref[:, j * R : (j + 1) * R] = jnp.where(rows == primal[one], weight[one], none)
        part = jnp.where(part_rows == local[one], weight[one], none)
        images.append(image_of(schur_ref[j], part))
    image = jnp.concatenate(images, axis=0)
    for at in range(0, NC, 256):
        rows = slice(at, at + 256)
        tile_ref[rows] = jnp.dot(basis_ref[rows], image, preferred_element_type=F32)


def image_of(schur, part):
    return lax.dot_general(
        schur, part, (((1,), (1,)), ((), ())), preferred_element_type=F32
    ).astype(BF16)


def second_kernel(schur_ref, basis_ref, image_ref, up_ref):
    at = pl.ds(pl.multiple_of(core() * HALF, HALF), HALF)
    for j in range(schur_ref.shape[0]):
        part = basis_ref[at, j * R : (j + 1) * R]
        image_ref[j * R : (j + 1) * R] = image_of(schur_ref[j], part)
    up_ref[...] = jnp.dot(basis_ref[:HALF], image_ref[...], preferred_element_type=F32)


def upper_kernel(own_ref, other_ref, token_ref, *outs):
    for d, out in enumerate(outs):
        at = slice(d * PIECE, (d + 1) * PIECE)
        out[...] = own_ref[at] + other_ref[at]
    token_ref[...] = outs[0][:8, :BLK]


def lower_kernel(basis_ref, image_ref, other_ref, _, *outs):
    down = jnp.dot(basis_ref[HALF:], image_ref[...], preferred_element_type=F32)
    for d, out in enumerate(outs):
        at = slice(d * PIECE, (d + 1) * PIECE)
        out[...] = down[at] + other_ref[HALF + d * PIECE : HALF + (d + 1) * PIECE]


def add_kernel(own_ref, other_ref, out_ref):
    out_ref[...] = own_ref[...] + other_ref[...]


def scale_kernel(*refs):
    count = NC // PIECE
    own, other = refs[:count], refs[count : 2 * count]
    out_ref, tile, sems = refs[2 * count :]

    def copy(d):
        at = pl.ds(d * PIECE, PIECE)
        return pltpu.make_async_copy(tile.at[at], out_ref.at[at], sems.at[d])

    down, across = [], []
    for d in range(count):
        total = jnp.abs(own[d][...]) + jnp.abs(other[d][...])
        mean = jnp.sum(total, axis=1, keepdims=True) / NC
        scale = jnp.broadcast_to(1.0 / jnp.sqrt(mean + 1e-06), (PIECE, BLK))
        down.append(scale[:, :1])
        across.append(scale.T[:1, :])
    halves = [jnp.concatenate(across[:2], axis=1), jnp.concatenate(across[2:], axis=1)]
    first = core() == 0
    mine = jnp.where(first, halves[0], halves[1])
    theirs = jnp.where(first, halves[1], halves[0])
    here = pl.ds(pl.multiple_of(core() * HALF, HALF), HALF)
    there = pl.ds(pl.multiple_of((1 - core()) * HALF, HALF), HALF)
    for d in range(count):
        at = slice(d * PIECE, (d + 1) * PIECE)
        tile[at, here] = own[d][...] * down[d] * mine
        tile[at, there] = other[d][...] * down[d] * theirs
        copy(d).start()
    for d in range(count):
        copy(d).wait()


def per_device(columns, line, coupling, local_block, counts, primal, partner):
    coupling, local_block, counts, primal = coupling[0], local_block[0], counts[0], primal[0]
    subs = coupling.shape[0]
    coupled_shape = ((subs, NI, R), BF16)

    def swap(a, axis, size, bit):
        return lax.ppermute(a, axis, [(i, i ^ bit) for i in range(size)])

    stiff, coupled = call(
        "diag",
        diag_kernel,
        [((subs, R), F32), coupled_shape],
        [ASPEC, ASPEC],
        [
            pltpu.VMEM((RB, subs, BLK, BLK), BF16),
            pltpu.SemaphoreType.DMA((RB,)),
            pltpu.SemaphoreType.DMA((HEAD,)),
        ],
    )(*in_hbm(local_block, coupling))
    def schur(first, last, here, stop, coupled):
        return call(
            "schur",
            functools.partial(schur_kernel, first, last, here, stop),
            [((last - first, R, R), BF16), coupled_shape],
            [SSPEC, ASPEC, VSPEC, VSPEC],
            [pltpu.SemaphoreType.DMA((max(stop - here, 1),))],
            {2: 1},
        )(counts, *in_hbm(coupling), *in_vmem(coupled, local_block))

    others = [swap(stiff, "gx", columns, d) for d in range(1, columns)]
    schur_all, _ = schur(0, subs, HEAD, subs, coupled)

    half, pieces = ((NC, HALF), F32), ((PIECE, HALF), F32)
    tile, basis = call(
        "first", first_kernel, [half, ((NC, subs * R), BF16)], [SSPEC] + [VSPEC] * (columns + 2)
    )(partner, primal, *in_vmem(stiff, *others, schur_all))
    tile = swap(tile, "gy", line, 1)
    image, up = call(
        "second",
        second_kernel,
        [((subs * R, HALF), BF16), ((HALF, HALF), F32)],
        [VSPEC] * 2,
    )(*in_vmem(schur_all, basis))
    count = HALF // PIECE
    token, *upper = call(
        "upper", upper_kernel, [((8, BLK), F32)] + [pieces] * count, [VSPEC] * 2
    )(*in_vmem(up, tile))
    token = swap(token, "gy", line, 1)
    lower = call("lower", lower_kernel, [pieces] * count, [VSPEC] * 4)(
        *in_vmem(basis, image, tile, token)
    )
    own = [*upper, *lower]

    add = call("add", add_kernel, [pieces], [VSPEC] * 2)
    steps = [2 << b for b in range((line // 2 - 1).bit_length())]
    for step in range(len(steps)):
        bits = steps[step], steps[-1 - step]
        for d in range(len(own)):
            hops = [(i, i ^ bits[(d ^ i) & 1]) for i in range(line)]
            (own[d],) = add(*in_vmem(own[d], lax.ppermute(own[d], "gy", hops)))
    other = [swap(piece, "gy", line, 1) for piece in own]
    result = pl.pallas_call(
        scale_kernel,
        out_shape=jax.ShapeDtypeStruct((NC, NC), F32),
        in_specs=[VSPEC] * (2 * len(own)),
        out_specs=ASPEC,
        scratch_shapes=[pltpu.VMEM((NC, NC), F32), pltpu.SemaphoreType.DMA((NC // BLK,))],
        compiler_params=pltpu.CompilerParams(vmem_limit_bytes=VMEM_LIMIT),
        name="scale",
    )(*in_vmem(*own, *other))
    return result[None]


def solution(mesh):
    placed = (
        P("gx", "gy", None, None),
        P("gx", "gy", None, None),
        P("gx", "gy"),
        P("gx", "gy", None),
        P(),
    )
    body = functools.partial(per_device, mesh.shape["gx"], mesh.shape["gy"])
    return jax.shard_map(
        body, mesh=mesh, in_specs=placed, out_specs=P("gx", None, None), check_vma=False
    )
```

```python
import functools

import jax
import jax.numpy as jnp
from jax import lax
from jax.experimental import pallas as pl
from jax.experimental.pallas import tpu as pltpu
from jax.sharding import PartitionSpec as P

BLK = 128
NC = 512
ROUNDS = 3
R = 512
NI = 1024
RB = 4
HEAD = 2
HALF = NC // 2
PIECE = 128
VMEM_LIMIT = 24 << 20

F32 = jnp.float32
BF16 = jnp.bfloat16


def in_vmem(*arrays):
    return [pltpu.with_memory_space_constraint(a, pltpu.VMEM) for a in arrays]


def in_hbm(*arrays):
    return [pltpu.with_memory_space_constraint(a, pltpu.HBM) for a in arrays]


VSPEC = pl.BlockSpec(memory_space=pltpu.VMEM)
SSPEC = pl.BlockSpec(memory_space=pltpu.SMEM)
ASPEC = pl.BlockSpec(memory_space=pl.ANY)


def call(name, kernel, outs, in_specs, scratch=(), aliases={}):
    shapes = tuple(pltpu.VMEM(shape, dtype) for shape, dtype in outs)
    return pl.pallas_call(
        kernel,
        out_shape=shapes,
        in_specs=in_specs,
        out_specs=(VSPEC,) * len(shapes),
        scratch_shapes=list(scratch),
        input_output_aliases=aliases,
        compiler_params=pltpu.CompilerParams(vmem_limit_bytes=VMEM_LIMIT),
        name=name,
    )


def diag_kernel(block_ref, coupling_ref, stiff_ref, coupled_ref, held, sems, head_sems):
    def copy(b):
        part = pl.ds(b * BLK, BLK)
        return pltpu.make_async_copy(block_ref.at[:, part, part], held.at[b], sems.at[b])

    def head(j):
        return pltpu.make_async_copy(coupling_ref.at[j], coupled_ref.at[j], head_sems.at[j])

    for b in range(RB):
        copy(b).start()
    for j in range(HEAD):
        head(j).start()
    shape = (BLK, BLK)
    on = lax.broadcasted_iota(jnp.int32, shape, 0) == lax.broadcasted_iota(jnp.int32, shape, 1)
    for b in range(RB):
        copy(b).wait()
        tile = held[b].astype(F32)
        stiff_ref[:, b * BLK : (b + 1) * BLK] = jnp.sum(jnp.where(on[None], tile, 0.0), axis=1)
    for j in range(HEAD):
        head(j).wait()


def put(live, gram, block, schur, row, col):
    for r in range(0, gram.shape[0], BLK):
        for q in range(0, gram.shape[1], BLK):
            at = slice(row + r, row + r + BLK), slice(col + q, col + q + BLK)
            value = block[at].astype(F32) - gram[r : r + BLK, q : q + BLK]
            last = max(row + r, col + q) // BLK
            if last > 0:
                value = jnp.where(live > last, value, 0.0)
            schur[at] = value.astype(BF16)


def schur_block(live, c, block, schur):
    half = R // 2
    dims = (((0,), (0,)), ((), ()))
    gram = lax.dot_general(c[:, :half], c[...], dims, preferred_element_type=F32)
    put(live, gram, block, schur, 0, 0)
    put(live, gram[:, half:].T, block, schur, half, 0)
    gram = lax.dot_general(c[:, half:], c[:, half:], dims, preferred_element_type=F32)
    put(live, gram, block, schur, half, half)


def schur_kernel(first, last, here, stop, counts_ref, coupling_ref, _, block_ref, schur_ref, coupled_ref, sems):
    def copy(j):
        return pltpu.make_async_copy(coupling_ref.at[j], coupled_ref.at[j], sems.at[j - here])

    def start(j, carry):
        copy(j).start()
        return carry

    def wait(j, carry):
        copy(j).wait()
        return carry

    def pair(p, carry):
        j = first + 2 * p
        if last > here:
            @pl.when(j >= here)
            def _():
                copy(j).wait()
                copy(j + 1).wait()

        for k in range(2):
            schur_block(counts_ref[j + k], coupled_ref.at[j + k], block_ref.at[j + k], schur_ref.at[j + k - first])
        return carry

    lax.fori_loop(here, stop, start, 0)
    lax.fori_loop(0, (last - first) // 2, pair, 0)
    lax.fori_loop(max(here, last), stop, wait, 0)


def core():
    return lax.axis_index("gy") & 1


def first_kernel(partner_ref, primal_ref, stiff_ref, *refs):
    *others, schur_ref, tile_ref, basis_ref = refs
    subs = schur_ref.shape[0]
    column = lax.axis_index("gx")
    mine = stiff_ref[...]
    total = mine
    for d, other in enumerate(others, 1):
        times = jnp.int32(0)
        for r in range(ROUNDS):
            times += (partner_ref[r, column] == (column ^ d)).astype(jnp.int32)
        total = total + times.astype(F32) * other[...]
    weight = (mine / total).astype(BF16)
    primal = primal_ref[...]
    rows = lax.broadcasted_iota(jnp.int32, (NC, R), 0).astype(jnp.int16)
    part_rows = rows[:HALF]
    local = (primal - (1 - core()) * HALF).astype(jnp.int16)
    primal = primal.astype(jnp.int16)
    none = jnp.zeros((), BF16)
    images = []
    for j in range(subs):
        one = slice(j, j + 1)
        basis_ref[:, j * R : (j + 1) * R] = jnp.where(rows == primal[one], weight[one], none)
        part = jnp.where(part_rows == local[one], weight[one], none)
        images.append(image_of(schur_ref[j], part))
    image = jnp.concatenate(images, axis=0)
    for at in range(0, NC, 256):
        rows = slice(at, at + 256)
        tile_ref[rows] = jnp.dot(basis_ref[rows], image, preferred_element_type=F32)


def image_of(schur, part):
    return lax.dot_general(
        schur, part, (((1,), (1,)), ((), ())), preferred_element_type=F32
    ).astype(BF16)


def second_kernel(schur_ref, basis_ref, image_ref, up_ref):
    at = pl.ds(pl.multiple_of(core() * HALF, HALF), HALF)
    for j in range(schur_ref.shape[0]):
        part = basis_ref[at, j * R : (j + 1) * R]
        image_ref[j * R : (j + 1) * R] = image_of(schur_ref[j], part)
    up_ref[...] = jnp.dot(basis_ref[:HALF], image_ref[...], preferred_element_type=F32)


def upper_kernel(own_ref, other_ref, token_ref, *outs):
    for d, out in enumerate(outs):
        at = slice(d * PIECE, (d + 1) * PIECE)
        out[...] = own_ref[at] + other_ref[at]
    token_ref[...] = outs[0][:8, :BLK]


def lower_kernel(basis_ref, image_ref, other_ref, _, *outs):
    down = jnp.dot(basis_ref[HALF:], image_ref[...], preferred_element_type=F32)
    for d, out in enumerate(outs):
        at = slice(d * PIECE, (d + 1) * PIECE)
        out[...] = down[at] + other_ref[HALF + d * PIECE : HALF + (d + 1) * PIECE]


def add_kernel(own_ref, other_ref, out_ref):
    out_ref[...] = own_ref[...] + other_ref[...]


def scale_kernel(*refs):
    count = NC // PIECE
    own, other = refs[:count], refs[count : 2 * count]
    out_ref, tile, sems = refs[2 * count :]

    def copy(d):
        at = pl.ds(d * PIECE, PIECE)
        return pltpu.make_async_copy(tile.at[at], out_ref.at[at], sems.at[d])

    down, across = [], []
    for d in range(count):
        total = jnp.abs(own[d][...]) + jnp.abs(other[d][...])
        mean = jnp.sum(total, axis=1, keepdims=True) / NC
        scale = jnp.broadcast_to(1.0 / jnp.sqrt(mean + 1e-06), (PIECE, BLK))
        down.append(scale[:, :1])
        across.append(scale.T[:1, :])
    halves = [jnp.concatenate(across[:2], axis=1), jnp.concatenate(across[2:], axis=1)]
    first = core() == 0
    mine = jnp.where(first, halves[0], halves[1])
    theirs = jnp.where(first, halves[1], halves[0])
    here = pl.ds(pl.multiple_of(core() * HALF, HALF), HALF)
    there = pl.ds(pl.multiple_of((1 - core()) * HALF, HALF), HALF)
    for d in range(count):
        at = slice(d * PIECE, (d + 1) * PIECE)
        tile[at, here] = own[d][...] * down[d] * mine
        tile[at, there] = other[d][...] * down[d] * theirs
        copy(d).start()
    for d in range(count):
        copy(d).wait()


def per_device(columns, line, coupling, local_block, counts, primal, partner):
    coupling, local_block, counts, primal = coupling[0], local_block[0], counts[0], primal[0]
    subs = coupling.shape[0]
    coupled_shape = ((subs, NI, R), BF16)

    def swap(a, axis, size, bit):
        return lax.ppermute(a, axis, [(i, i ^ bit) for i in range(size)])

    stiff, coupled = call(
        "diag",
        diag_kernel,
        [((subs, R), F32), coupled_shape],
        [ASPEC, ASPEC],
        [
            pltpu.VMEM((RB, subs, BLK, BLK), BF16),
            pltpu.SemaphoreType.DMA((RB,)),
            pltpu.SemaphoreType.DMA((HEAD,)),
        ],
    )(*in_hbm(local_block, coupling))
    def schur(first, last, here, stop, coupled):
        return call(
            "schur",
            functools.partial(schur_kernel, first, last, here, stop),
            [((last - first, R, R), BF16), coupled_shape],
            [SSPEC, ASPEC, VSPEC, VSPEC],
            [pltpu.SemaphoreType.DMA((max(stop - here, 1),))],
            {2: 1},
        )(counts, *in_hbm(coupling), *in_vmem(coupled, local_block))

    others = [swap(stiff, "gx", columns, d) for d in range(1, columns)]
    schur_all, _ = schur(0, subs, HEAD, subs, coupled)

    half, pieces = ((NC, HALF), F32), ((PIECE, HALF), F32)
    tile, basis = call(
        "first", first_kernel, [half, ((NC, subs * R), BF16)], [SSPEC] + [VSPEC] * (columns + 2)
    )(partner, primal, *in_vmem(stiff, *others, schur_all))
    tile = swap(tile, "gy", line, 1)
    image, up = call(
        "second",
        second_kernel,
        [((subs * R, HALF), BF16), ((HALF, HALF), F32)],
        [VSPEC] * 2,
    )(*in_vmem(schur_all, basis))
    count = HALF // PIECE
    token, *upper = call(
        "upper", upper_kernel, [((8, BLK), F32)] + [pieces] * count, [VSPEC] * 2
    )(*in_vmem(up, tile))
    token = swap(token, "gy", line, 1)
    lower = call("lower", lower_kernel, [pieces] * count, [VSPEC] * 4)(
        *in_vmem(basis, image, tile, token)
    )
    own = [*upper, *lower]

    add = call("add", add_kernel, [pieces], [VSPEC] * 2)
    steps = [2 << b for b in range((line // 2 - 1).bit_length())]
    for step in range(len(steps)):
        pair = steps[step], steps[-1 - step]
        for d in range(len(own)):
            hops = [(i, i ^ pair[(d // 2 ^ d) & 1]) for i in range(line)]
            (own[d],) = add(*in_vmem(own[d], lax.ppermute(own[d], "gy", hops)))
    other = [swap(piece, "gy", line, 1) for piece in own]
    result = pl.pallas_call(
        scale_kernel,
        out_shape=jax.ShapeDtypeStruct((NC, NC), F32),
        in_specs=[VSPEC] * (2 * len(own)),
        out_specs=ASPEC,
        scratch_shapes=[pltpu.VMEM((NC, NC), F32), pltpu.SemaphoreType.DMA((NC // BLK,))],
        compiler_params=pltpu.CompilerParams(vmem_limit_bytes=VMEM_LIMIT),
        name="scale",
    )(*in_vmem(*own, *other))
    return result[None]


def solution(mesh):
    placed = (
        P("gx", "gy", None, None),
        P("gx", "gy", None, None),
        P("gx", "gy"),
        P("gx", "gy", None),
        P(),
    )
    body = functools.partial(per_device, mesh.shape["gx"], mesh.shape["gy"])
    return jax.shard_map(
        body, mesh=mesh, in_specs=placed, out_specs=P("gx", None, None), check_vma=False
    )
```
